768 devices in a mesh: chord: 48 (over y_hi, z, core), span: 16 (over y_lo, x).
Axes of the slice: x: 4, y: 8 (y_hi: 2, y_lo: 4; y = y_hi * 4 + y_lo), z: 12, core: 2. Of those that a mesh axis runs over, the one named last changes fastest.
Arguments:
- velocity: float32 [3, 192, 64, 1024], P(None, 'chord', 'span'), may hold values from -6 to 6
- pressure: float32 [192, 64, 1024], P('chord', 'span'), may hold values from -6 to 6
- viscosity: float32 [192, 64, 1024], P('chord', 'span'), may hold values from 0.02 to 0.15
- send_list: int32 [2304, 2], P('chord'), may hold values from -1 to 15, as said below
- recv_slot: int32 [192, 4], P('chord'), may hold values from 0 to 95, as said below
- marker_block: int32 [98304], P('chord'), may hold values from 0 to 3
- marker_cells: int32 [16, 98304], P(None, 'chord'), may hold values from 0 to 1023, as said below
- marker_layer: int32 [98304], P('chord'), may hold values from 0 to 63, as said below
- marker_frac: float32 [98304], P('chord'), may hold values from 0 to 1
- marker_weights: float32 [16, 98304], P(None, 'chord'), may hold values from 0.15 to 0.5
- marker_target: float32 [3, 98304], P(None, 'chord'), may hold values from -3 to 3
- marker_count: int32 [48], P('chord'), may hold values from 1 to 128, as said below
Outputs:
- velocity_next: float32 [3, 192, 64, 1024], P(None, 'chord', 'span')
- pressure_next: float32 [192, 64, 1024], P('chord', 'span')
The draws below stay inside these ranges and needn't reach their ends.
Inputs may be any that keep to these rules, and one draw needn't show every extreme that they name: `send_list`: row d times the number of chord indices plus e lists, in 2 slots, the edges that chord index d sends to chord index e, each as 4 * block + side, -1 in empty slots. Every block has one neighbour across each side, the relation is symmetric (across the opposite side), and the pattern is the same on every chord index up to a shift of chord indices. Some pair of chord indices fills all 2 slots. `recv_slot`: entry (block, side) is the source chord index times 2 plus the slot of the edge that forms that side's ghost row; that edge is the listed entry of the source's row for this chord index. `marker_cells`: the 16 support cells of a marker form a 4 x 4 square of its block's plane, listed row by row. `marker_layer`: the marker slots of a chord index come in groups of 128, one group for each span index in order; the lowest support layer of group g's markers lies in layers g * 4 to (g + 1) * 4 - 1. `marker_count`: A marker is live when its position within its group is below its chord index's count.
All inputs are finite; a program needn't handle non-finite values.
Results may differ from the reference program's by a relative error of at most 0.0001.
Values sent between devices are 32-bit elements; how exact they have to be, the bound alone decides.
No kernel may reach another device: no remote copies, remote signals or barrier semaphores. Data moves between devices by JAX's collectives and lax.ppermute only.
A program may use at most 64 MiB of HBM per device.

```python
import math
import jax
import jax.numpy as jnp

EDGE = 32
SUPPORT = 4
CELLS = 1024
PATCH = 16
NB = 4
SZ = 4
MS = 2048
ITERS = 8
NBLK = 192
NZ = 64
NMARK = 98304
GROUP = 128
FCAP = 2


def faces_layout(key):
    chords = NBLK // NB
    halfway = chords // 2
    remaining = 2 * NB - FCAP - 1
    classes = jnp.repeat(jnp.arange(2, halfway, dtype=jnp.int32), FCAP)
    classes = jax.random.permutation(jax.random.fold_in(key, 11), classes)[:remaining]
    picked = jnp.concatenate([jnp.ones((FCAP,), jnp.int32), jnp.full((1,), halfway, jnp.int32), classes])
    picked = jax.random.permutation(jax.random.fold_in(key, 12), picked)
    sign_flip = 2 * jax.random.randint(jax.random.fold_in(key, 13), (2 * NB,), 0, 2) - 1
    shifts = picked * sign_flip
    first_shift = shifts[:NB]
    second_shift = shifts[NB:]
    offsets = jnp.stack([-first_shift, first_shift, -second_shift, second_shift], axis=1).reshape(4 * NB) % chords
    entries = jnp.arange(4 * NB, dtype=jnp.int32)
    same_offset = offsets[:, None] == offsets[None, :]
    earlier = entries[None, :] < entries[:, None]
    slot_rank = jnp.sum(jnp.where(same_offset & earlier, 1, 0), axis=1).astype(jnp.int32)
    table = jnp.full((chords, FCAP), -1, jnp.int32).at[offsets, slot_rank].set(entries)
    devices = jnp.arange(chords, dtype=jnp.int32)
    relative = (devices[None, :] - devices[:, None]) % chords
    send_list = table[relative].reshape(chords * chords, FCAP)
    partner = entries ^ 1
    source = (devices[:, None] - offsets[partner][None, :]) % chords
    recv_slot = (source * FCAP + slot_rank[partner][None, :]).reshape(chords * NB, 4)
    return (send_list.astype(jnp.int32), recv_slot.astype(jnp.int32))


def draw_send_list(key, part):
    return faces_layout(key)[0]


def draw_recv_slot(key, part):
    return faces_layout(key)[1]


def draw_marker_block(key, part):
    key = jax.random.fold_in(key, 21)
    marker_slot = jnp.arange(NMARK, dtype=jnp.int32)
    chosen = jax.random.randint(key, (NMARK,), 0, NB)
    return jnp.where(marker_slot == 1, NB - 1, jnp.where(marker_slot == 0, 0, chosen)).astype(jnp.int32)


def draw_marker_cells(key, part):
    key = jax.random.fold_in(key, 22)
    marker_slot = jnp.arange(NMARK, dtype=jnp.int32)
    corner = jax.random.randint(key, (2, NMARK), 0, EDGE - SUPPORT + 1)
    corner = jnp.where(marker_slot[None, :] == 1, EDGE - SUPPORT, jnp.where(marker_slot[None, :] == 0, 0, corner))
    support_step = jnp.arange(SUPPORT, dtype=jnp.int32)
    first_coord = corner[0][None, None, :] + support_step[:, None, None]
    second_coord = corner[1][None, None, :] + support_step[None, :, None]
    return (first_coord * EDGE + second_coord).reshape(SUPPORT * SUPPORT, NMARK).astype(jnp.int32)


def draw_marker_layer(key, part):
    key = jax.random.fold_in(key, 23)
    marker_slot = jnp.arange(NMARK, dtype=jnp.int32)
    within = marker_slot % MS % GROUP
    group_index = marker_slot % MS // GROUP
    offset_draw = jax.random.randint(key, (NMARK,), 0, SZ)
    offset_draw = jnp.where(within == 0, SZ - 1, jnp.where(within == 1, 0, offset_draw))
    return (group_index * SZ + offset_draw).astype(jnp.int32)


def draw_marker_count(key, part):
    key = jax.random.fold_in(key, 24)
    chords = NMARK // MS
    first_draw = jax.random.randint(jax.random.fold_in(key, 1), (chords,), 1, GROUP + 1)
    second_draw = jax.random.randint(jax.random.fold_in(key, 2), (chords,), 1, GROUP + 1)
    busiest = jax.random.randint(jax.random.fold_in(key, 3), (), 0, chords)
    counts = jnp.minimum(first_draw, second_draw)
    return jnp.where(jnp.arange(chords, dtype=jnp.int32) == busiest, GROUP, counts).astype(jnp.int32)


def levels(key, shape, cuts, smallest, largest):
    def one(dim, parts):
        steps = jax.random.uniform(jax.random.fold_in(jax.random.fold_in(key, 6), dim), (parts,), jnp.float32, smallest / len(cuts), largest / len(cuts))
        return jnp.repeat(jnp.exp(steps), shape[dim] // parts).reshape((-1,) + (1,) * (len(shape) - dim - 1))

    loudness = one(*cuts[0])
    for cut in cuts[1:]:
        loudness = loudness * one(*cut)
    return loudness


def gaussian(own_key, shape, width, reach, shards=(), held_as=jnp.bfloat16):
    array = width * jax.random.normal(own_key, shape, jnp.float32)
    if shards:
        array = array * levels(own_key, shape, shards, -0.22, 0.18)
    return jnp.clip(array, -reach, reach).astype(held_as)


def setup_inputs(seed: int = 0) -> dict:
    seeds = jax.random.split(jax.random.key(seed), 13)
    velocity = gaussian(seeds[0], (3, NBLK, NZ, CELLS), 1.0, 6.0, ((1, 48), (2, 16)), jnp.float32)
    pressure = gaussian(seeds[1], (NBLK, NZ, CELLS), 1.0, 6.0, ((0, 48), (1, 16)), jnp.float32)
    viscosity = jnp.clip(jnp.exp(math.log(0.15) - 2.014903 * jax.random.uniform(seeds[2], (NBLK, NZ, CELLS), jnp.float32) ** levels(seeds[2], (NBLK, NZ, CELLS), ((0, 48), (1, 16)), -0.2, 0.2)), 0.02, 0.15)
    send_list = draw_send_list(jax.random.fold_in(seeds[12], 71), 0)
    recv_slot = draw_recv_slot(jax.random.fold_in(seeds[12], 71), 0)
    marker_block = draw_marker_block(jax.random.fold_in(seeds[12], 71), 0)
    marker_cells = draw_marker_cells(jax.random.fold_in(seeds[12], 71), 0)
    marker_layer = draw_marker_layer(jax.random.fold_in(seeds[12], 71), 0)
    marker_frac = jnp.clip(1.0 * jax.random.uniform(seeds[8], (NMARK,), jnp.float32) ** levels(seeds[8], (NMARK,), ((0, 48),), -0.2, 0.2), 0.0, 1.0)
    marker_weights = jnp.clip(0.15 + 0.35 * jax.random.uniform(seeds[9], (PATCH, NMARK), jnp.float32) ** levels(seeds[9], (PATCH, NMARK), ((1, 48),), -0.2, 0.2), 0.15, 0.5)
    marker_target = gaussian(seeds[10], (3, NMARK), 0.5, 3.0, ((1, 48),), jnp.float32)
    marker_count = draw_marker_count(jax.random.fold_in(seeds[12], 71), 0)
    return dict(velocity=velocity, pressure=pressure, viscosity=viscosity, send_list=send_list, recv_slot=recv_slot, marker_block=marker_block, marker_cells=marker_cells, marker_layer=marker_layer, marker_frac=marker_frac, marker_weights=marker_weights, marker_target=marker_target, marker_count=marker_count)


def edge_rows(cell_field):
    plane_grid = cell_field.reshape(cell_field.shape[:-1] + (EDGE, EDGE))
    return jnp.stack([plane_grid[..., 0, :], plane_grid[..., EDGE - 1, :], plane_grid[..., :, 0], plane_grid[..., :, EDGE - 1]], axis=-2)


def four_sides(cell_field, ghost_rows):
    plane_grid = cell_field.reshape(cell_field.shape[:-1] + (EDGE, EDGE))
    west_side = jnp.concatenate([ghost_rows[..., 0:1, :], plane_grid[..., :-1, :]], axis=-2)
    east_side = jnp.concatenate([plane_grid[..., 1:, :], ghost_rows[..., 1:2, :]], axis=-2)
    south_side = jnp.concatenate([jnp.swapaxes(ghost_rows[..., 2:3, :], -1, -2), plane_grid[..., :, :-1]], axis=-1)
    north_side = jnp.concatenate([plane_grid[..., :, 1:], jnp.swapaxes(ghost_rows[..., 3:4, :], -1, -2)], axis=-1)
    return tuple(each_side.reshape(cell_field.shape) for each_side in (west_side, east_side, south_side, north_side))


def span_weights(fraction):
    distance = jnp.stack([1.0 + fraction, fraction, 1.0 - fraction, 2.0 - fraction])
    return 0.25 * (1.0 + jnp.cos((0.5 * math.pi) * distance))


def beside_all(cell_field, neighbour_block, neighbour_side):
    all_edges = edge_rows(cell_field)
    picked = all_edges[neighbour_block, :, neighbour_side, :]
    ghost_rows = jnp.transpose(picked, (0, 2, 1, 3))
    return four_sides(cell_field, ghost_rows) + (jnp.roll(cell_field, 1, axis=1), jnp.roll(cell_field, -1, axis=1))


def reference(velocity, pressure, viscosity, send_list, recv_slot, marker_block, marker_cells, marker_layer, marker_frac, marker_weights, marker_target, marker_count):
    chords = NBLK // NB
    block_ids = jnp.arange(NBLK, dtype=jnp.int32)
    source = recv_slot // FCAP
    entry_id = send_list[source * chords + (block_ids // NB)[:, None], recv_slot % FCAP]
    neighbour_block = source * NB + entry_id // 4
    neighbour_side = entry_id % 4

    tilde_velocity = []
    for component in range(3):
        around_cells = beside_all(velocity[component], neighbour_block, neighbour_side)
        laplace = around_cells[0] + around_cells[1] + around_cells[2] + around_cells[3] + around_cells[4] + around_cells[5] - 6.0 * velocity[component]
        tilde_velocity.append(velocity[component] + viscosity * laplace)

    marker_slot = jnp.arange(NMARK, dtype=jnp.int32)
    owner_index = marker_slot // MS
    live_mask = jnp.where((marker_slot % MS) % GROUP < marker_count[owner_index], 1.0, 0.0).astype(jnp.float32)
    kernel = span_weights(marker_frac)[:, None, :] * marker_weights[None, :, :]
    support_step = jnp.arange(SUPPORT, dtype=jnp.int32)
    layer_index = (marker_layer[None, :] + support_step[:, None]) % NZ
    block_index = owner_index * NB + marker_block
    point_index = (block_index[None, None, :] * NZ + layer_index[:, None, :]) * CELLS + marker_cells[None, :, :]
    star_velocity = []
    for component in range(3):
        flat_tilde = tilde_velocity[component].reshape(-1)
        sampled = jnp.sum(kernel * flat_tilde[point_index], axis=(0, 1))
        force_all = live_mask * (marker_target[component] - sampled)
        spread = flat_tilde.at[point_index].add(kernel * force_all[None, None, :])
        star_velocity.append(spread.reshape(tilde_velocity[component].shape))

    first_sides = beside_all(star_velocity[0], neighbour_block, neighbour_side)
    second_sides = beside_all(star_velocity[1], neighbour_block, neighbour_side)
    third_sides = beside_all(star_velocity[2], neighbour_block, neighbour_side)
    divergence = 0.5 * ((first_sides[1] - first_sides[0]) + (second_sides[3] - second_sides[2]) + (third_sides[5] - third_sides[4]))

    current = pressure
    for sweep_index in range(ITERS):
        around_cells = beside_all(current, neighbour_block, neighbour_side)
        current = (around_cells[0] + around_cells[1] + around_cells[2] + around_cells[3] + around_cells[4] + around_cells[5] - divergence) / 6.0
    around_cells = beside_all(current, neighbour_block, neighbour_side)
    gradients = [around_cells[1] - around_cells[0], around_cells[3] - around_cells[2], around_cells[5] - around_cells[4]]
    velocity_next = jnp.stack([star_velocity[component] - 0.5 * gradients[component] for component in range(3)])
    return velocity_next, current
```

```python
import math

import jax
import jax.numpy as jnp
import ml_dtypes
import numpy as np
from jax import lax
from jax.experimental import pallas as pl
from jax.experimental.pallas import tpu as pltpu
from jax.sharding import PartitionSpec as P

EDGE = 32
CELLS = EDGE * EDGE
NB = 4
SZ = 4
DEPTH = 3
STRIDE = 40
WIDTH = 1536
LANES = 128
SEG = 4 * LANES
F32 = jnp.float32
BF16 = jnp.bfloat16


def place_of(i, k):
    return STRIDE * (i + DEPTH) + k + 4


def edge_cell(side, depth, x):
    return [(depth, x), (EDGE - 1 - depth, x), (x, depth), (x, EDGE - 1 - depth)][side]


def ghost_cell(side, depth, x):
    return [(-1 - depth, x), (EDGE + depth, x), (x, -1 - depth), (x, EDGE + depth)][side]


def pack_matrix(rows, where):
    table = np.zeros((rows, SEG), np.float32)
    for side in range(4):
        for depth in range(DEPTH):
            for x in range(EDGE):
                table[where(*edge_cell(side, depth, x)), side * LANES + depth * EDGE + x] = 1
        for corner in range(4):
            for cell in range(4):
                i, k = cell // 2, cell % 2
                i = i if corner // 2 == 0 else EDGE - 1 - i
                k = k if corner % 2 == 0 else EDGE - 1 - k
                table[where(i, k), side * LANES + 96 + corner * 4 + cell] = 1
    return table.astype(ml_dtypes.bfloat16)


def place_matrix():
    table = np.zeros((SEG, WIDTH), np.float32)
    for side in range(4):
        for depth in range(DEPTH):
            for x in range(EDGE):
                table[side * LANES + depth * EDGE + x, place_of(*ghost_cell(side, depth, x))] = 1
    for vertex in range(4):
        for cell in range(3):
            i, k = cell // 2, cell % 2
            i = -1 - i if vertex // 2 == 0 else EDGE + i
            k = -1 - k if vertex % 2 == 0 else EDGE + k
            table[vertex * LANES + 96 + cell, place_of(i, k)] = 1
    return table.astype(ml_dtypes.bfloat16)


def rim_matrix():
    table = np.zeros((CELLS, LANES), np.float32)
    for side in range(4):
        for x in range(EDGE):
            i, k = edge_cell(side, 0, x)
            table[i * EDGE + k, side * EDGE + x] = 1
    return table.astype(ml_dtypes.bfloat16)


def sheet_mask():
    mask = np.zeros((8, WIDTH), np.float32)
    for i in range(-DEPTH, EDGE + DEPTH):
        for k in range(-DEPTH, EDGE + DEPTH):
            inside_i, inside_k = 0 <= i < EDGE, 0 <= k < EDGE
            if inside_i and not inside_k:
                mask[:4, place_of(i, k)] = 1
            if inside_k and not inside_i:
                mask[4:, place_of(i, k)] = 1
    return mask


def block_mask():
    mask = np.zeros((8, WIDTH), np.float32)
    for i in range(EDGE):
        mask[:, place_of(i, 0) : place_of(i, 0) + EDGE] = 1
    return mask


def vertex_place(vertex):
    return place_of(-1 if vertex // 2 == 0 else EDGE, -1 if vertex % 2 == 0 else EDGE)


def pick(x, table):
    high = x.astype(BF16)
    rest = x - high.astype(F32)
    middle = rest.astype(BF16)
    low = (rest - middle.astype(F32)).astype(BF16)
    parts = jnp.dot(jnp.concatenate([high, middle, low], axis=0), table, preferred_element_type=F32)
    rows = x.shape[0]
    return (parts[:rows] + parts[rows : 2 * rows]) + parts[2 * rows :]


def shifted(x, lanes):
    return pltpu.roll(x, lanes % x.shape[1], axis=1)


def lane_ids(rows):
    return lax.broadcasted_iota(jnp.int32, (rows, LANES), 1)


def remap(x, width, pieces):
    rows = x.shape[0]
    lane = lane_ids(rows)
    out = []
    for tile in range(width // LANES):
        acc = jnp.zeros((rows, LANES), F32)
        base = tile * LANES
        for src, dst in pieces:
            first, last = max(dst, base), min(dst + EDGE, base + LANES)
            while first < last:
                at = src + first - dst
                column = at // LANES
                stop = min(last, first + (column + 1) * LANES - at)
                value = x[:, column * LANES : (column + 1) * LANES]
                turn = (first - base - at % LANES) % LANES
                if turn:
                    value = pltpu.roll(value, turn, axis=1)
                acc = jnp.where((lane >= first - base) & (lane < stop - base), value, acc)
                first = stop
        out.append(acc)
    return jnp.concatenate(out, axis=1)


def expand(x):
    return remap(x, WIDTH, [(EDGE * i, place_of(i, 0)) for i in range(EDGE)])


def compact(x):
    return remap(x, CELLS, [(place_of(i, 0), EDGE * i) for i in range(EDGE)])


def store_table(strips, table_ref, field, fields, first_row):
    lane = lane_ids(NB)
    for layer in range(SZ):
        for side in range(4):
            rows = strips[layer, first_row : first_row + NB, side * LANES : (side + 1) * LANES]
            turned = pltpu.roll(rows, 16, axis=1)
            for slot in range(2):
                low = jnp.broadcast_to(rows[2 * slot : 2 * slot + 1], rows.shape)
                high = jnp.broadcast_to(turned[2 * slot + 1 : 2 * slot + 2], rows.shape)
                value = jnp.where(lane < 96, rows, jnp.where(lane < 112, low, high))
                for block in range(NB):
                    entry = (slot * fields + field) * 16 + block * 4 + side
                    at = slot * SZ + layer
                    table_ref[entry, at : at + 1, :] = value[block : block + 1]


def post(send_ref, table_ref, out_ref, fields, count):
    def one(target, carry):
        first = jnp.maximum(send_ref[2 * target], 0)
        second = jnp.maximum(send_ref[2 * target + 1], 0)
        for field in range(fields):
            out_ref[target * fields + field] = (
                table_ref[field * 16 + first] + table_ref[(fields + field) * 16 + second]
            )
        return carry

    lax.fori_loop(0, count, one, 0, unroll=4)


def first_pack(send_ref, cells_ref, p_ref, rim_ref, pack_ref, out_ref, table_ref, strips_ref):
    count = out_ref.shape[0] // 2
    table_ref[...] = jnp.zeros(table_ref.shape, F32)
    rims = pick(cells_ref[...].reshape(SZ * 16, CELLS), rim_ref[...])
    lane = lane_ids(NB)
    for layer in range(SZ):
        rows = rims[layer * 16 : (layer + 1) * 16]
        for side in range(4):
            value = jnp.zeros((NB, LANES), F32)
            for comp in range(3):
                part = rows[comp * NB : (comp + 1) * NB]
                turn = EDGE * (comp - side) % LANES
                if turn:
                    part = pltpu.roll(part, turn, axis=1)
                value = jnp.where(lane // EDGE == comp, part, value)
            for block in range(NB):
                for slot in range(2):
                    at = slot * SZ + layer
                    table_ref[slot * 32 + block * 4 + side, at : at + 1, :] = value[block : block + 1]
    strips_ref[...] = pick(p_ref[...].reshape(SZ * 8, CELLS), pack_ref[...]).reshape(SZ, 8, SEG)
    store_table(strips_ref, table_ref, 1, 2, 0)
    post(send_ref, table_ref, out_ref, 2, count)


class Hops:
    def __init__(self, me_ref, send_ref, recv_ref, near_ref, count):
        self.me, self.recv, self.near, self.count = me_ref[0], recv_ref, near_ref, count
        for edge in range(16):
            source, slot = recv_ref[edge] // 2, recv_ref[edge] % 2
            back = lax.rem(2 * self.me - source + count, count)
            near_ref[edge] = send_ref[2 * back + slot] // 4
            near_ref[16 + edge] = lax.rem(source - self.me + count, count)

    def rows(self, block, side):
        entry = self.recv[block * 4 + side]
        return entry // 2, entry % 2

    def hop(self, block, offset, side):
        edge = block * 4 + side
        return self.near[edge], offset + self.near[16 + edge]

    def source(self, offset):
        return lax.rem(self.me + offset, self.count)


def near_rows(got_ref, source, slot, field, fields):
    rows = got_ref[source * fields + field]
    return jnp.where(slot == 1, pltpu.roll(rows, SZ, axis=0), rows)


def patch_rows(got_ref, hops, block, offset, corner, field, fields, target, cell):
    rows = near_rows(got_ref, hops.source(offset), block // 2, field, fields)
    lane = 96 + (block % 2) * 16 + corner * 4 + cell
    return pltpu.roll(rows, lax.rem(target - lane + 2 * LANES, LANES), axis=1)


def gather_ghosts(got_ref, hops, ghost_ref, field, fields):
    lane = lane_ids(8)
    for block in range(NB):
        for vertex in range(4):
            strip = near_rows(got_ref, *hops.rows(block, vertex), field, fields)
            i_side, k_side = vertex // 2, 2 + vertex % 2
            far = (1 - vertex // 2) * 2 + 1 - vertex % 2
            for sheet, (side, then) in enumerate(((i_side, k_side), (k_side, i_side))):
                at, offset = hops.hop(block, 0, side)
                at, offset = hops.hop(at, offset, then)
                second = patch_rows(got_ref, hops, at, offset, far, field, fields, 96, 0)
                at, offset = hops.hop(at, offset, side ^ 1)
                beyond = far ^ 2 if sheet == 0 else far ^ 1
                third = patch_rows(got_ref, hops, at, offset, beyond, field, fields, 100, 0)
                value = jnp.where(
                    lane < 96, strip, jnp.where(lane < 100, second, jnp.where(lane == 100, third, 0.0))
                )
                row = sheet * NB + block
                for layer in range(SZ):
                    ghost_ref[layer, row : row + 1, vertex * LANES : (vertex + 1) * LANES] = value[
                        layer : layer + 1
                    ]


def third_cells(ghosts):
    lane = lane_ids(8)
    tiles = [jnp.zeros((8, LANES), F32) for _ in range(WIDTH // LANES)]
    for vertex in range(4):
        tile, at = vertex_place(vertex) // LANES, vertex_place(vertex) % LANES
        value = pltpu.roll(ghosts[:, vertex * LANES : (vertex + 1) * LANES], (at - 100) % LANES, axis=1)
        tiles[tile] = jnp.where(lane == at, value, tiles[tile])
    return jnp.concatenate(tiles, axis=1)


def vertex_masks():
    lane = lax.broadcasted_iota(jnp.int32, (8, WIDTH), 1)
    first = lax.broadcasted_iota(jnp.int32, (8, WIDTH), 0) < NB
    places = [vertex_place(v) for v in range(4)]
    west = first & ((lane == places[0]) | (lane == places[1]))
    east = first & ((lane == places[2]) | (lane == places[3]))
    south = ~first & ((lane == places[0]) | (lane == places[2]))
    north = ~first & ((lane == places[1]) | (lane == places[3]))
    return west, east, south, north


def corrections(ext, third):
    west, east, south, north = vertex_masks()
    return (
        jnp.where(west, third - shifted(ext, -STRIDE), 0.0),
        jnp.where(east, third - shifted(ext, STRIDE), 0.0),
        jnp.where(south, third - shifted(ext, -1), 0.0),
        jnp.where(north, third - shifted(ext, 1), 0.0),
    )


def merge(x, mask):
    return jnp.where(mask, pltpu.roll(x, NB, axis=0), x)


def second_halves(x):
    return jnp.concatenate([x, x], axis=0)


def unpack_pressure(own, got_ref, hops, ghost_ref, place_ref, own_ref, corr_ref, field, fields, up, down):
    gather_ghosts(got_ref, hops, ghost_ref, field, fields)
    placed = pick(ghost_ref[...].reshape(SZ * 8, SEG), place_ref[...])
    for layer in range(SZ):
        ext = own(layer) + placed[layer * 8 : (layer + 1) * 8]
        own_ref[layer] = ext
        corr_ref[layer] = sum(corrections(ext, third_cells(ghost_ref[layer])))
        if layer >= 1:
            up[layer - 1, :, :WIDTH] = ext
        if layer < SZ - 1:
            down[layer, :, :WIDTH] = ext


def first_unpack(
    me_ref, send_ref, recv_ref, got_ref, p_ref, place_ref, own_ref, corr_ref, rim_ref, up_ref, down_ref, ghost_ref, near_ref
):
    count = got_ref.shape[0] // 2
    hops = Hops(me_ref, send_ref, recv_ref, near_ref, count)
    lane = lane_ids(8)
    for block in range(NB):
        strips = [near_rows(got_ref, *hops.rows(block, side), 0, 2) for side in range(4)]
        for comp in range(4):
            value = jnp.zeros((8, LANES), F32)
            if comp < 3:
                for side in range(4):
                    turn = EDGE * (side - comp) % LANES
                    part = pltpu.roll(strips[side], turn, axis=1) if turn else strips[side]
                    value = jnp.where(lane // EDGE == side, part, value)
            row = comp * NB + block
            for layer in range(SZ):
                rim_ref[layer, row : row + 1, :] = value[layer : layer + 1]
    unpack_pressure(
        lambda layer: expand(p_ref[layer]), got_ref, hops, ghost_ref, place_ref, own_ref, corr_ref, 1, 2, up_ref, down_ref
    )
    for layer in range(SZ):
        for half in range(2):
            rows = rim_ref[layer, half * 8 : (half + 1) * 8, :]
            at = WIDTH + half * LANES
            if layer >= 1:
                up_ref[layer - 1, :, at : at + LANES] = rows
            if layer < SZ - 1:
                down_ref[layer, :, at : at + LANES] = rows


def later_unpack(
    me_ref, send_ref, recv_ref, got_ref, p_ref, place_ref, block_ref, own_ref, corr_ref, up_ref, down_ref, ghost_ref, near_ref
):
    count = got_ref.shape[0]
    hops = Hops(me_ref, send_ref, recv_ref, near_ref, count)
    unpack_pressure(
        lambda layer: jnp.where(block_ref[...] > 0.0, p_ref[layer], 0.0),
        got_ref, hops, ghost_ref, place_ref, own_ref, corr_ref, 0, 1, up_ref, down_ref,
    )


def rim_rows(ref, layer):
    return jnp.concatenate([ref[layer, :, WIDTH : WIDTH + LANES], ref[layer, :, WIDTH + LANES :]], axis=0)


def forcing(
    send_ref, count_ref, own_ref, low_ref, high_ref, rim_ref, rim_low_ref, rim_high_ref, spread_ref, pack_ref,
    start_ref, block_ref, corner_ref, phi_ref, weight_ref, target_ref,
    star_ref, out_ref, tilde_ref, plane_ref, table_ref, strips_ref,
):
    markers = start_ref.shape[1]
    group = markers // 2
    layers = SZ + 2 * (SZ - 1)
    cell = lax.broadcasted_iota(jnp.int32, (16, CELLS), 1)

    def cells_at(layer):
        if layer < 0:
            return low_ref[layer + SZ]
        return own_ref[layer] if layer < SZ else high_ref[layer - SZ]

    def rims_at(layer):
        if layer < 0:
            return rim_rows(rim_low_ref, layer + SZ - 1)
        return rim_ref[layer] if layer < SZ else rim_rows(rim_high_ref, layer - SZ)

    for at in range(layers):
        layer = at - (SZ - 1)
        here = cells_at(layer)
        around = jnp.where(cell >= EDGE, shifted(here, EDGE), 0.0)
        around += jnp.where(cell < CELLS - EDGE, shifted(here, -EDGE), 0.0)
        around += jnp.where(cell % EDGE != 0, shifted(here, 1), 0.0)
        around += jnp.where(cell % EDGE != EDGE - 1, shifted(here, -1), 0.0)
        around += pick(rims_at(layer), spread_ref[...])
        around += cells_at(layer - 1) + cells_at(layer + 1)
        eddy = second_halves(second_halves(here[3 * NB :]))
        tilde_ref[at] = here + eddy * (around - 6.0 * here)
    row_i = corner_ref[...] // EDGE
    row_k = corner_ref[...] % EDGE
    along = lax.broadcasted_iota(jnp.int32, (EDGE, markers), 0)
    lines = []
    for a in range(4):
        line = jnp.zeros((EDGE, markers), F32)
        for b in range(4):
            line = jnp.where(along == row_k + b, weight_ref[4 * a + b : 4 * a + b + 1, :], line)
        lines.append(line)

    def fill(i, carry):
        value = jnp.zeros((EDGE, markers), F32)
        for a in range(4):
            value = jnp.where(row_i + a == i, lines[a], value)
        plane_ref[pl.ds(i * EDGE, EDGE), :] = value
        return carry

    lax.fori_loop(0, EDGE, fill, 0)
    start = start_ref[...]

    def span_weight(layer):
        value = jnp.zeros((1, markers), F32)
        for a in range(4):
            value = jnp.where(start + a == layer, phi_ref[a : a + 1, :], value)
        return value

    weights = [span_weight(at - (SZ - 1)) for at in range(layers)]
    dots = jnp.dot(
        tilde_ref[...].reshape(layers * 16, CELLS), plane_ref[...],
        precision=lax.Precision.HIGHEST, preferred_element_type=F32,
    )
    total = jnp.zeros((16, markers), F32)
    for at in range(layers):
        total += weights[at] * dots[at * 16 : (at + 1) * 16]
    mine = (lax.broadcasted_iota(jnp.int32, (16, markers), 0) % NB) == block_ref[...]
    total = jnp.where(mine, total, 0.0)
    place = lax.broadcasted_iota(jnp.int32, (1, markers), 1) % group
    live = place < count_ref[0]
    rows = []
    for comp in range(3):
        sampled = jnp.sum(total[comp * NB : (comp + 1) * NB], axis=0, keepdims=True)
        force = jnp.where(live, target_ref[comp : comp + 1, :] - sampled, 0.0)
        rows.append(jnp.broadcast_to(force, (NB, markers)))
    rows.append(jnp.zeros((NB, markers), F32))
    force = jnp.where(mine, jnp.concatenate(rows, axis=0), 0.0)
    pushes = jnp.concatenate([weights[layer + SZ - 1] * force for layer in range(SZ)], axis=0)
    spread = lax.dot_general(
        pushes, plane_ref[...], (((1,), (1,)), ((), ())),
        precision=lax.Precision.HIGHEST, preferred_element_type=F32,
    )
    star = tilde_ref[SZ - 1 : 2 * SZ - 1].reshape(SZ * 16, CELLS) + spread
    star_ref[...] = star.reshape(SZ, 16, CELLS)
    table_ref[...] = jnp.zeros(table_ref.shape, F32)
    strips_ref[...] = pick(star, pack_ref[...]).reshape(SZ, 16, SEG)
    for comp in range(3):
        store_table(strips_ref, table_ref, comp, 3, comp * NB)
    post(send_ref, table_ref, out_ref, 3, out_ref.shape[0] // 3)


def star_unpack(
    me_ref, send_ref, recv_ref, got_ref, star_ref, place_ref, mask_ref, flat_ref, third_ref, up_ref, down_ref, ghost_ref, near_ref
):
    count = got_ref.shape[0] // 3
    hops = Hops(me_ref, send_ref, recv_ref, near_ref, count)
    for comp in range(3):
        gather_ghosts(got_ref, hops, ghost_ref.at[comp], comp, 3)
    placed = pick(ghost_ref[...].reshape(3 * SZ * 8, SEG), place_ref[...])
    mask = mask_ref[...] > 0.0
    for layer in range(SZ):
        whole = expand(star_ref[layer])
        exts = []
        for comp in range(3):
            at = (comp * SZ + layer) * 8
            exts.append(second_halves(whole[comp * NB : (comp + 1) * NB]) + placed[at : at + 8])
        west, east, _, _ = corrections(exts[0], third_cells(ghost_ref[0, layer]))
        _, _, south, north = corrections(exts[1], third_cells(ghost_ref[1, layer]))
        spread = shifted(exts[0], -STRIDE) - shifted(exts[0], STRIDE)
        spread += shifted(exts[1], -1) - shifted(exts[1], 1)
        spread += (west - east) + (south - north)
        flat = merge(0.5 * spread, mask)
        flat_ref[layer] = flat
        third_ref[layer] = exts[2]
        if layer >= 2:
            up_ref[layer - 2] = flat
        if layer >= 1:
            up_ref[layer + 1] = exts[2]
        if layer < 2:
            down_ref[layer] = flat
        if layer < 3:
            down_ref[layer + 2] = exts[2]


def sweep(source, target, first, last, rhs_ref, corr_ref, mask):
    for at in range(first, last):
        here = source[at]
        around = (shifted(here, STRIDE) + shifted(here, -STRIDE)) + (shifted(here, 1) + shifted(here, -1))
        around += source[at - 1] + source[at + 1]
        around -= rhs_ref[at - 1]
        if corr_ref is not None and DEPTH <= at < DEPTH + SZ:
            around += corr_ref[at - DEPTH]
        target[at] = merge(around * (1.0 / 6.0), mask)


def load_layers(work_ref, own_ref, low_ref, high_ref):
    for layer in range(DEPTH):
        work_ref[layer] = low_ref[layer, :, :WIDTH]
        work_ref[DEPTH + SZ + layer] = high_ref[layer, :, :WIDTH]
    for layer in range(SZ):
        work_ref[DEPTH + layer] = own_ref[layer]


def three_sweeps(work_ref, other_ref, rhs_ref, corr_ref, mask):
    sweep(work_ref, other_ref, 1, 9, rhs_ref, corr_ref, mask)
    sweep(other_ref, work_ref, 2, 8, rhs_ref, None, mask)
    sweep(work_ref, other_ref, 3, 7, rhs_ref, None, mask)


def send_pressure(send_ref, done_ref, pack_ref, p_ref, out_ref, table_ref, strips_ref):
    p_ref[...] = done_ref[DEPTH : DEPTH + SZ]
    table_ref[...] = jnp.zeros(table_ref.shape, F32)
    strips_ref[...] = pick(p_ref[...].reshape(SZ * 8, WIDTH), pack_ref[...]).reshape(SZ, 8, SEG)
    store_table(strips_ref, table_ref, 0, 1, 0)
    post(send_ref, table_ref, out_ref, 1, out_ref.shape[0])


def first_sweeps(
    send_ref, own_ref, corr_ref, low_ref, high_ref, flat_ref, third_ref, star_low_ref, star_high_ref, mask_ref, pack_ref,
    p_ref, rhs_ref, out_ref, work_ref, other_ref, table_ref, strips_ref,
):
    mask = mask_ref[...] > 0.0
    load_layers(work_ref, own_ref, low_ref, high_ref)

    def flat_at(layer):
        if layer < 0:
            return star_low_ref[layer + 2]
        return flat_ref[layer] if layer < SZ else star_high_ref[layer - SZ]

    def third_at(layer):
        if layer < 0:
            return star_low_ref[layer + 5]
        return third_ref[layer] if layer < SZ else star_high_ref[layer - SZ + 2]

    for layer in range(-2, SZ + 2):
        rhs_ref[layer + 2] = flat_at(layer) + 0.5 * (third_at(layer + 1) - third_at(layer - 1))
    three_sweeps(work_ref, other_ref, rhs_ref, corr_ref, mask)
    send_pressure(send_ref, other_ref, pack_ref, p_ref, out_ref, table_ref, strips_ref)


def later_sweeps(
    send_ref, own_ref, corr_ref, low_ref, high_ref, rhs_ref, mask_ref, pack_ref,
    p_ref, out_ref, work_ref, other_ref, table_ref, strips_ref,
):
    load_layers(work_ref, own_ref, low_ref, high_ref)
    three_sweeps(work_ref, other_ref, rhs_ref, corr_ref, mask_ref[...] > 0.0)
    send_pressure(send_ref, other_ref, pack_ref, p_ref, out_ref, table_ref, strips_ref)


def last_sweeps(own_ref, corr_ref, low_ref, high_ref, rhs_ref, mask_ref, star_ref, out_ref, work_ref, other_ref):
    mask = mask_ref[...] > 0.0
    load_layers(work_ref, own_ref, low_ref, high_ref)
    sweep(work_ref, other_ref, 1, 9, rhs_ref, corr_ref, mask)
    sweep(other_ref, work_ref, 2, 8, rhs_ref, None, mask)
    for layer in range(SZ):
        here = work_ref[DEPTH + layer]
        rows = [
            shifted(here, -STRIDE) - shifted(here, STRIDE),
            shifted(here, -1) - shifted(here, 1),
            work_ref[DEPTH + layer + 1] - work_ref[DEPTH + layer - 1],
            here,
        ]
        flat = compact(jnp.concatenate([row[:NB] for row in rows], axis=0))
        star = star_ref[layer]
        row = lax.broadcasted_iota(jnp.int32, (16, CELLS), 0)
        out_ref[layer] = jnp.where(row < 3 * NB, star - 0.5 * flat, flat)


def call(kernel, name, out_shapes, scratch, scalars):
    smem, vmem = pl.BlockSpec(memory_space=pltpu.SMEM), pl.BlockSpec(memory_space=pltpu.VMEM)
    shapes = tuple(jax.ShapeDtypeStruct(shape, F32) for shape in out_shapes)

    def run(*args):
        return pl.pallas_call(
            kernel,
            name=name,
            out_shape=shapes,
            in_specs=[smem if at < scalars else vmem for at in range(len(args))],
            out_specs=tuple(vmem for _ in shapes),
            scratch_shapes=scratch,
            compiler_params=pltpu.CompilerParams(vmem_limit_bytes=24 << 20),
        )(*args)

    return run


def trade(messages, count):
    whole = messages.reshape(count, -1, LANES)
    got = lax.all_to_all(whole, "chord", split_axis=0, concat_axis=0, tiled=True)
    return got.reshape(messages.shape)


def beside(up, down):
    size = lax.axis_size("span")
    low = lax.ppermute(up, "span", [(i, (i + 1) % size) for i in range(size)])
    high = lax.ppermute(down, "span", [(i, (i + size - 1) % size) for i in range(size)])
    return low, high


def local(
    velocity,
    pressure,
    viscosity,
    send_list,
    recv_slot,
    marker_block,
    marker_cells,
    marker_layer,
    marker_frac,
    marker_weights,
    marker_target,
    marker_count,
):
    count, strips = lax.axis_size("chord"), lax.axis_size("span")
    me = lax.axis_index("chord").astype(jnp.int32).reshape(1)
    at = lax.axis_index("span").astype(jnp.int32)
    send, recv = send_list.reshape(-1), recv_slot.reshape(-1)
    rim, spread = jnp.asarray(RIM), jnp.asarray(RIM.T)
    pack_flat, pack_ext = jnp.asarray(PACK_FLAT), jnp.asarray(PACK_EXT)
    place, mask, inside = jnp.asarray(PLACE), jnp.asarray(MASK), jnp.asarray(INSIDE)
    cells = jnp.concatenate([velocity, viscosity[None]], axis=0)
    cells = jnp.transpose(cells, (2, 0, 1, 3)).reshape(SZ, 16, CELLS)
    by_layer = jnp.transpose(pressure, (1, 0, 2))
    flat_p = jnp.concatenate([by_layer, by_layer], axis=1)

    plane, flat = (SZ, 8, WIDTH), (SZ, 16, CELLS)
    tables = lambda fields: pltpu.VMEM((2 * fields * 16, 8, LANES), F32)
    strip_rows = lambda rows: pltpu.VMEM((SZ, rows, SEG), F32)
    near = pltpu.SMEM((32,), jnp.int32)
    layers = pltpu.VMEM((SZ + 2 * DEPTH, 8, WIDTH), F32)

    cells_low, cells_high = beside(cells, cells)
    (messages,) = call(first_pack, "first_pack", [(2 * count, 8, LANES)], [tables(2), strip_rows(8)], 1)(
        send, cells, flat_p, rim, pack_flat
    )
    got = trade(messages, count)
    edge = (DEPTH, 8, WIDTH + 2 * LANES)
    own, corr, rims, up, down = call(
        first_unpack, "first_unpack", [plane, plane, (SZ, 16, LANES), edge, edge], [strip_rows(8), near], 3
    )(me, send, recv, got, flat_p, place)
    low, high = beside(up, down)

    group = marker_block.shape[0] // strips
    below = (at + strips - 1) % strips

    def two_groups(values):
        axis = values.ndim - 1
        parts = [lax.dynamic_slice_in_dim(values, g * group, group, axis=axis) for g in (at, below)]
        return jnp.concatenate(parts, axis=axis)

    first = jnp.concatenate([jnp.full((group,), at * SZ), jnp.full((group,), (below + 1) * SZ)])
    start = two_groups(marker_layer) - first
    fraction = two_groups(marker_frac)
    distance = jnp.stack([1.0 + fraction, fraction, 1.0 - fraction, 2.0 - fraction])
    phi = 0.25 * (1.0 + jnp.cos(0.5 * math.pi * distance))
    star, messages = call(
        forcing, "forcing", [flat, (3 * count, 8, LANES)],
        [
            pltpu.VMEM((SZ + 2 * DEPTH, 16, CELLS), F32),
            pltpu.VMEM((CELLS, 2 * group), F32),
            tables(3),
            strip_rows(16),
        ],
        2,
    )(
        send, marker_count, cells, cells_low, cells_high, rims, low, high, spread, pack_flat,
        start[None], two_groups(marker_block)[None], two_groups(marker_cells[:1]), phi,
        two_groups(marker_weights), two_groups(marker_target),
    )
    got = trade(messages, count)
    edge = (5, 8, WIDTH)
    flat_part, third, up, down = call(
        star_unpack, "star_unpack", [plane, plane, edge, edge], [pltpu.VMEM((3, SZ, 8, SEG), F32), near], 3
    )(me, send, recv, got, star, place, mask)
    star_low, star_high = beside(up, down)

    p, rhs, messages = call(
        first_sweeps, "first_sweeps", [plane, (SZ + 4, 8, WIDTH), (count, 8, LANES)],
        [layers, layers, tables(1), strip_rows(8)], 1,
    )(send, own, corr, low, high, flat_part, third, star_low, star_high, mask, pack_ext)
    edge = (DEPTH, 8, WIDTH)
    for last in (False, True):
        got = trade(messages, count)
        own, corr, up, down = call(
            later_unpack, "later_unpack", [plane, plane, edge, edge], [strip_rows(8), near], 3
        )(me, send, recv, got, p, place, inside)
        low, high = beside(up, down)
        if not last:
            p, messages = call(
                later_sweeps, "later_sweeps", [plane, (count, 8, LANES)], [layers, layers, tables(1), strip_rows(8)], 1
            )(send, own, corr, low, high, rhs, mask, pack_ext)
    (out,) = call(last_sweeps, "last_sweeps", [flat], [layers, layers], 0)(
        own, corr, low, high, rhs, mask, star
    )
    out = jnp.transpose(out.reshape(SZ, 4, NB, CELLS), (1, 2, 0, 3))
    return out[:3], out[3]


RIM = rim_matrix()
PACK_FLAT = pack_matrix(CELLS, lambda i, k: EDGE * i + k)
PACK_EXT = pack_matrix(WIDTH, place_of)
PLACE = place_matrix()
MASK = sheet_mask()
INSIDE = block_mask()


def solution(mesh):
    in_specs = (
        P(None, "chord", "span", None),
        P("chord", "span", None),
        P("chord", "span", None),
        P("chord", None),
        P("chord", None),
        P("chord"),
        P(None, "chord"),
        P("chord"),
        P("chord"),
        P(None, "chord"),
        P(None, "chord"),
        P("chord"),
    )
    out_specs = (P(None, "chord", "span", None), P("chord", "span", None))
    return jax.shard_map(local, mesh=mesh, in_specs=in_specs, out_specs=out_specs, check_vma=False)
```

```python
import math

import jax
import jax.numpy as jnp
import ml_dtypes
import numpy as np
from jax import lax
from jax.experimental import pallas as pl
from jax.experimental.pallas import tpu as pltpu
from jax.sharding import PartitionSpec as P

EDGE = 32
CELLS = EDGE * EDGE
NB = 4
SZ = 4
DEPTH = 3
STRIDE = 40
WIDTH = 1536
LANES = 128
SEG = 4 * LANES
F32 = jnp.float32
BF16 = jnp.bfloat16


def place_of(i, k):
    return STRIDE * (i + DEPTH) + k + 4


def edge_cell(side, depth, x):
    return [(depth, x), (EDGE - 1 - depth, x), (x, depth), (x, EDGE - 1 - depth)][side]


def ghost_cell(side, depth, x):
    return [(-1 - depth, x), (EDGE + depth, x), (x, -1 - depth), (x, EDGE + depth)][side]


def pack_matrix(rows, where):
    table = np.zeros((rows, SEG), np.float32)
    for side in range(4):
        for depth in range(DEPTH):
            for x in range(EDGE):
                table[where(*edge_cell(side, depth, x)), side * LANES + depth * EDGE + x] = 1
        for corner in range(4):
            for cell in range(4):
                i, k = cell // 2, cell % 2
                i = i if corner // 2 == 0 else EDGE - 1 - i
                k = k if corner % 2 == 0 else EDGE - 1 - k
                table[where(i, k), side * LANES + 96 + corner * 4 + cell] = 1
    return table.astype(ml_dtypes.bfloat16)


def place_matrix():
    table = np.zeros((SEG, WIDTH), np.float32)
    for side in range(4):
        for depth in range(DEPTH):
            for x in range(EDGE):
                table[side * LANES + depth * EDGE + x, place_of(*ghost_cell(side, depth, x))] = 1
    for vertex in range(4):
        for cell in range(3):
            i, k = cell // 2, cell % 2
            i = -1 - i if vertex // 2 == 0 else EDGE + i
            k = -1 - k if vertex % 2 == 0 else EDGE + k
            table[vertex * LANES + 96 + cell, place_of(i, k)] = 1
    return table.astype(ml_dtypes.bfloat16)


def spread_matrix():
    table = np.zeros((SEG, WIDTH), np.float32)
    for side in range(4):
        for depth in range(2):
            for x in range(EDGE):
                table[side * LANES + depth * EDGE + x, place_of(*ghost_cell(side, depth, x))] = 1
        for x in range(EDGE):
            table[side * LANES + 2 * EDGE + x, place_of(*edge_cell(side, 0, x))] = 0.5 if side % 2 else -0.5
    for vertex in range(4):
        lane = vertex * LANES + 96
        i, k = vertex_cell(vertex)
        in_i, in_k = (1, 1) if vertex == 0 else (1, -1) if vertex == 1 else (-1, 1) if vertex == 2 else (-1, -1)
        table[lane, place_of(i, k)] = 1
        table[lane + 1, place_of(i, k + in_k)] = -0.5 * in_k
        table[lane + 2, place_of(i - in_i, k + in_k)] = -0.5 * in_k
        table[lane + 3, place_of(i + in_i, k)] = -0.5 * in_i
        table[lane + 4, place_of(i + in_i, k - in_k)] = -0.5 * in_i
        table[lane + 5, place_of(i, k)] = 0.5 * in_i
        table[lane + 6, place_of(i, k)] = 0.5 * in_k
    return table.astype(ml_dtypes.bfloat16)


def rim_matrix():
    table = np.zeros((CELLS, LANES), np.float32)
    for side in range(4):
        for x in range(EDGE):
            i, k = edge_cell(side, 0, x)
            table[i * EDGE + k, side * EDGE + x] = 1
    return table.astype(ml_dtypes.bfloat16)


def sheet_mask():
    mask = np.zeros((8, WIDTH), np.float32)
    for i in range(-DEPTH, EDGE + DEPTH):
        for k in range(-DEPTH, EDGE + DEPTH):
            inside_i, inside_k = 0 <= i < EDGE, 0 <= k < EDGE
            if inside_i and not inside_k:
                mask[:4, place_of(i, k)] = 1
            if inside_k and not inside_i:
                mask[4:, place_of(i, k)] = 1
    return mask


def block_mask():
    mask = np.zeros((8, WIDTH), np.float32)
    for i in range(EDGE):
        mask[:, place_of(i, 0) : place_of(i, 0) + EDGE] = 1
    return mask


def vertex_cell(vertex):
    return -1 if vertex // 2 == 0 else EDGE, -1 if vertex % 2 == 0 else EDGE


def vertex_place(vertex):
    return place_of(*vertex_cell(vertex))


def pick(x, table):
    high = x.astype(BF16)
    rest = x - high.astype(F32)
    middle = rest.astype(BF16)
    low = (rest - middle.astype(F32)).astype(BF16)
    parts = jnp.dot(jnp.concatenate([high, middle, low], axis=0), table, preferred_element_type=F32)
    rows = x.shape[0]
    return (parts[:rows] + parts[rows : 2 * rows]) + parts[2 * rows :]


def shifted(x, lanes):
    return pltpu.roll(x, lanes % x.shape[1], axis=1)


def lane_ids(rows):
    return lax.broadcasted_iota(jnp.int32, (rows, LANES), 1)


def remap(x, width, pieces):
    rows = x.shape[0]
    lane = lane_ids(rows)
    out = []
    for tile in range(width // LANES):
        acc = jnp.zeros((rows, LANES), F32)
        base = tile * LANES
        for src, dst in pieces:
            first, last = max(dst, base), min(dst + EDGE, base + LANES)
            while first < last:
                at = src + first - dst
                column = at // LANES
                stop = min(last, first + (column + 1) * LANES - at)
                value = x[:, column * LANES : (column + 1) * LANES]
                turn = (first - base - at % LANES) % LANES
                if turn:
                    value = pltpu.roll(value, turn, axis=1)
                acc = jnp.where((lane >= first - base) & (lane < stop - base), value, acc)
                first = stop
        out.append(acc)
    return jnp.concatenate(out, axis=1)


def expand(x):
    return remap(x, WIDTH, [(EDGE * i, place_of(i, 0)) for i in range(EDGE)])


def compact(x):
    return remap(x, CELLS, [(place_of(i, 0), EDGE * i) for i in range(EDGE)])


def store_table(rows_of, table_ref, field, fields):
    lane = lane_ids(NB)
    for layer in range(SZ):
        for side in range(4):
            rows = rows_of(layer, side)
            turned = pltpu.roll(rows, 16, axis=1)
            for slot in range(2):
                low = jnp.broadcast_to(rows[2 * slot : 2 * slot + 1], rows.shape)
                high = jnp.broadcast_to(turned[2 * slot + 1 : 2 * slot + 2], rows.shape)
                value = jnp.where(lane < 96, rows, jnp.where(lane < 112, low, high))
                for block in range(NB):
                    entry = (slot * fields + field) * 16 + block * 4 + side
                    at = slot * SZ + layer
                    table_ref[entry, at : at + 1, :] = value[block : block + 1]


def segments(strips, row):
    return lambda layer, side: strips[layer, row : row + NB, side * LANES : (side + 1) * LANES]


def post(send_ref, table_ref, out_ref, fields, count):
    def one(target, carry):
        first = jnp.maximum(send_ref[0, target], 0)
        second = jnp.maximum(send_ref[1, target], 0)
        for field in range(fields):
            out_ref[target * fields + field] = (
                table_ref[field * 16 + first] + table_ref[(fields + field) * 16 + second]
            )
        return carry

    lax.fori_loop(0, count, one, 0, unroll=4)


def first_pack(
    send_any, velocity_any, p_any, rim_any, pack_any, out_ref,
    send_ref, velocity_ref, p_ref, rim_ref, pack_ref, table_ref, done_ref,
):
    copies = [
        pltpu.make_async_copy(source, target, done_ref.at[at])
        for at, (source, target) in enumerate(
            (
                (velocity_any, velocity_ref), (rim_any, rim_ref), (p_any, p_ref), (pack_any, pack_ref), (send_any, send_ref),
            )
        )
    ]
    for copy in copies:
        copy.start()
    table_ref[...] = jnp.zeros(table_ref.shape, F32)
    lane = lane_ids(SZ)
    copies[0].wait()
    copies[1].wait()
    rims = pick(velocity_ref[...].reshape(3 * NB * SZ, CELLS), rim_ref[...])
    for block in range(NB):
        for side in range(4):
            value = jnp.zeros((SZ, LANES), F32)
            for comp in range(3):
                first = (comp * NB + block) * SZ
                part = rims[first : first + SZ]
                turn = EDGE * (comp - side) % LANES
                if turn:
                    part = pltpu.roll(part, turn, axis=1)
                value = jnp.where(lane // EDGE == comp, part, value)
            for slot in range(2):
                table_ref[slot * 32 + block * 4 + side, slot * SZ : (slot + 1) * SZ, :] = value
    copies[2].wait()
    copies[3].wait()
    strips = pick(p_ref[...].reshape(NB * SZ, CELLS), pack_ref[...])
    for side in range(4):
        parts = [strips[block * SZ : (block + 1) * SZ, side * LANES : (side + 1) * LANES] for block in range(NB)]
        for slot in range(2):
            patch = jnp.where(lane < 112, parts[2 * slot], pltpu.roll(parts[2 * slot + 1], 16, axis=1))
            for block in range(NB):
                value = jnp.where(lane < 96, parts[block], patch)
                table_ref[slot * 32 + 16 + block * 4 + side, slot * SZ : (slot + 1) * SZ, :] = value
    copies[4].wait()
    post(send_ref, table_ref, out_ref, 2, out_ref.shape[0] // 2)


def routes(me_ref, send_ref, recv_ref, out_ref, near_ref):
    me, count = me_ref[0], send_ref.shape[1]
    for edge in range(16):
        block, side = edge // 4, edge % 4
        entry = recv_ref[block, side]
        source, slot = entry // 2, entry % 2
        out_ref[2 * edge], out_ref[2 * edge + 1] = source, slot
        back = lax.rem(2 * me - source + count, count)
        near_ref[edge] = send_ref[slot, back] // 4
        near_ref[16 + edge] = lax.rem(source - me + count, count)
    for block in range(NB):
        for vertex in range(4):
            i_side, k_side = vertex // 2, 2 + vertex % 2
            for sheet, (side, then) in enumerate(((i_side, k_side), (k_side, i_side))):
                at, offset = block, 0
                for step, across in enumerate((side, then, side ^ 1)):
                    edge = at * 4 + across
                    at, offset = near_ref[edge], offset + near_ref[16 + edge]
                    place = route_at(block, vertex, sheet, step)
                    out_ref[place] = lax.rem(me + offset, count)
                    out_ref[place + 1] = at // 2
                    out_ref[place + 2] = 96 + (at % 2) * 16


def route_at(block, vertex, sheet, step):
    return 32 + (((block * 4 + vertex) * 2 + sheet) * 3 + step) * 3


ROUTES = 32 + 32 * 9


def near_rows(got_ref, source, slot, field, fields):
    rows = got_ref[source * fields + field]
    return jnp.where(slot == 1, pltpu.roll(rows, SZ, axis=0), rows)


def strip_rows_of(got_ref, route_ref, block, side, field, fields):
    edge = block * 4 + side
    return near_rows(got_ref, route_ref[2 * edge], route_ref[2 * edge + 1], field, fields)


def patch_rows(got_ref, route_ref, place, corner, field, fields, target, cell):
    rows = near_rows(got_ref, route_ref[place], route_ref[place + 1], field, fields)
    turn = target - (corner * 4 + cell) + 2 * LANES - route_ref[place + 2]
    return pltpu.roll(rows, lax.rem(turn, LANES), axis=1)


def gather_ghosts(got_ref, route_ref, ghost_ref, field, fields):
    lane = lane_ids(8)
    for block in range(NB):
        for vertex in range(4):
            strip = strip_rows_of(got_ref, route_ref, block, vertex, field, fields)
            far = (1 - vertex // 2) * 2 + 1 - vertex % 2
            for sheet in range(2):
                twice, thrice = (route_at(block, vertex, sheet, step) for step in (1, 2))
                second = patch_rows(got_ref, route_ref, twice, far, field, fields, 96, 0)
                beyond = far ^ 2 if sheet == 0 else far ^ 1
                third = patch_rows(got_ref, route_ref, thrice, beyond, field, fields, 100, 0)
                value = jnp.where(
                    lane < 96, strip, jnp.where(lane < 100, second, jnp.where(lane == 100, third, 0.0))
                )
                row = sheet * NB + block
                for layer in range(SZ):
                    ghost_ref[layer, row : row + 1, vertex * LANES : (vertex + 1) * LANES] = value[
                        layer : layer + 1
                    ]


def third_cells(ghosts):
    lane = lane_ids(8)
    tiles = [jnp.zeros((8, LANES), F32) for _ in range(WIDTH // LANES)]
    for vertex in range(4):
        tile, at = vertex_place(vertex) // LANES, vertex_place(vertex) % LANES
        value = pltpu.roll(ghosts[:, vertex * LANES : (vertex + 1) * LANES], (at - 100) % LANES, axis=1)
        tiles[tile] = jnp.where(lane == at, value, tiles[tile])
    return jnp.concatenate(tiles, axis=1)


def vertex_masks():
    lane = lax.broadcasted_iota(jnp.int32, (8, WIDTH), 1)
    first = lax.broadcasted_iota(jnp.int32, (8, WIDTH), 0) < NB
    places = [vertex_place(v) for v in range(4)]
    west = first & ((lane == places[0]) | (lane == places[1]))
    east = first & ((lane == places[2]) | (lane == places[3]))
    south = ~first & ((lane == places[0]) | (lane == places[2]))
    north = ~first & ((lane == places[1]) | (lane == places[3]))
    return west, east, south, north


def corrections(ext, third):
    west, east, south, north = vertex_masks()
    return (
        jnp.where(west, third - shifted(ext, -STRIDE), 0.0),
        jnp.where(east, third - shifted(ext, STRIDE), 0.0),
        jnp.where(south, third - shifted(ext, -1), 0.0),
        jnp.where(north, third - shifted(ext, 1), 0.0),
    )


def fold(ext):
    lane, last = lane_ids(NB), ext[:NB, WIDTH - LANES :]
    for vertex in range(4):
        tile, at = vertex_place(vertex) // LANES * LANES, vertex_place(vertex) % LANES
        value = pltpu.roll(ext[NB:, tile : tile + LANES], (112 + vertex - at) % LANES, axis=1)
        last = jnp.where(lane == 112 + vertex, value, last)
    return jnp.concatenate([ext[:NB, : WIDTH - LANES], last], axis=1)


def unfold(rows):
    lane, last = lane_ids(NB), rows[:, WIDTH - LANES : WIDTH]
    tiles = [rows[:, at : at + LANES] for at in range(0, WIDTH, LANES)]
    for vertex in range(4):
        tile, at = vertex_place(vertex) // LANES, vertex_place(vertex) % LANES
        value = pltpu.roll(last, (at - 112 - vertex) % LANES, axis=1)
        tiles[tile] = jnp.where(lane == at, value, tiles[tile])
    return jnp.concatenate([rows[:, :WIDTH], jnp.concatenate(tiles, axis=1)], axis=0)


def merge(x, mask):
    return jnp.where(mask, pltpu.roll(x, NB, axis=0), x)


def second_halves(x):
    return jnp.concatenate([x, x], axis=0)


def unpack_pressure(own, got_ref, route_ref, ghost_ref, place_ref, own_ref, corr_ref, field, fields, up, down):
    gather_ghosts(got_ref, route_ref, ghost_ref, field, fields)
    placed = pick(ghost_ref[...].reshape(SZ * 8, SEG), place_ref[...])
    for layer in range(SZ):
        ext = own(layer) + placed[layer * 8 : (layer + 1) * 8]
        own_ref[layer] = ext
        corr_ref[layer] = sum(corrections(ext, third_cells(ghost_ref[layer])))
        if layer >= 1:
            up[layer - 1, :, :WIDTH] = fold(ext)
        if layer < SZ - 1:
            down[layer, :, :WIDTH] = fold(ext)


def first_unpack(
    route_ref, got_ref, p_ref, place_ref, own_ref, corr_ref, rim_ref, up_ref, down_ref, ghost_ref, block_ref
):
    lane = lane_ids(8)
    for block in range(NB):
        strips = [strip_rows_of(got_ref, route_ref, block, side, 0, 2) for side in range(4)]
        for comp in range(4):
            value = jnp.zeros((8, LANES), F32)
            if comp < 3:
                for side in range(4):
                    turn = EDGE * (side - comp) % LANES
                    part = pltpu.roll(strips[side], turn, axis=1) if turn else strips[side]
                    value = jnp.where(lane // EDGE == side, part, value)
            row = comp * NB + block
            for layer in range(SZ):
                rim_ref[layer, row : row + 1, :] = value[layer : layer + 1]
    for block in range(NB):
        rows = expand(p_ref[block])
        for sheet in range(2):
            block_ref[:, sheet * NB + block, :] = rows
    unpack_pressure(
        lambda layer: block_ref[layer], got_ref, route_ref, ghost_ref, place_ref, own_ref, corr_ref, 1, 2, up_ref, down_ref
    )
    for layer in range(SZ):
        for comp in range(3):
            rows = rim_ref[layer, comp * NB : (comp + 1) * NB, :]
            at = WIDTH + comp * LANES
            if layer >= 1:
                up_ref[layer - 1, :, at : at + LANES] = rows
            if layer < SZ - 1:
                down_ref[layer, :, at : at + LANES] = rows


def later_unpack(
    route_ref, got_ref, p_ref, place_ref, block_ref, own_ref, corr_ref, up_ref, down_ref, ghost_ref
):
    unpack_pressure(
        lambda layer: jnp.where(block_ref[...] > 0.0, p_ref[layer], 0.0),
        got_ref, route_ref, ghost_ref, place_ref, own_ref, corr_ref, 0, 1, up_ref, down_ref,
    )


def rim_rows(ref, layer):
    rows = [ref[layer, :, at : at + LANES] for at in range(WIDTH, WIDTH + 3 * LANES, LANES)]
    return jnp.concatenate(rows + [jnp.zeros((NB, LANES), F32)], axis=0)


def weigh(
    at_ref, block_ref, cells_ref, layer_ref, fraction_ref, weight_ref, target_ref, plane_ref, span_ref, aim_ref
):
    group = plane_ref.shape[1] // 2
    along = lax.broadcasted_iota(jnp.int32, (EDGE, group), 0)
    for which in range(2):
        lanes = pl.ds(pl.multiple_of(at_ref[which] * group, group), group)
        here = slice(which * group, (which + 1) * group)
        corner = cells_ref[0:1, lanes]
        row_i, row_k = corner // EDGE, corner % EDGE
        weight = weight_ref[:, lanes]
        lines = []
        for a in range(4):
            line = jnp.zeros((EDGE, group), F32)
            for b in range(4):
                line = jnp.where(along == row_k + b, weight[4 * a + b : 4 * a + b + 1], line)
            lines.append(line)
        for i in range(EDGE):
            value = jnp.zeros((EDGE, group), F32)
            for a in range(4):
                value = jnp.where(row_i + a == i, lines[a], value)
            plane_ref[i * EDGE : (i + 1) * EDGE, here] = value
        start = layer_ref[:, lanes] - (at_ref[which] + which) * SZ
        fraction = fraction_ref[:, lanes]
        phi = [0.25 * (1.0 + jnp.cos(0.5 * math.pi * distance)) for distance in
               (1.0 + fraction, fraction, 1.0 - fraction, 2.0 - fraction)]
        for at in range(SZ + 2 * DEPTH):
            value = jnp.zeros((1, group), F32)
            for a in range(4):
                value = jnp.where(start + a == at - DEPTH, phi[a], value)
            span_ref[at : at + 1, here] = value
        aim_ref[0:3, here] = target_ref[:, lanes]
        aim_ref[3:4, here] = block_ref[:, lanes].astype(F32)


def diffused(cells_at, rims, spread, layer):
    cell = lax.broadcasted_iota(jnp.int32, (16, CELLS), 1)
    here = cells_at(layer)
    around = jnp.where(cell >= EDGE, shifted(here, EDGE), 0.0)
    around += jnp.where(cell < CELLS - EDGE, shifted(here, -EDGE), 0.0)
    around += jnp.where(cell % EDGE != 0, shifted(here, 1), 0.0)
    around += jnp.where(cell % EDGE != EDGE - 1, shifted(here, -1), 0.0)
    around += pick(rims, spread)
    around += cells_at(layer - 1) + cells_at(layer + 1)
    eddy = second_halves(second_halves(here[3 * NB :]))
    return here + eddy * (around - 6.0 * here)


def span_row(span_ref, layer):
    return span_ref[layer + DEPTH : layer + DEPTH + 1, :]


def layers_of(own_ref, low_ref, high_ref):
    def at(layer):
        if layer < 0:
            return low_ref[layer + SZ]
        return own_ref[layer] if layer < SZ else high_ref[layer - SZ]

    return at


def samples(tilde_ref, plane_ref, weights):
    dots = jnp.dot(
        tilde_ref[...].reshape(len(weights) * 16, CELLS), plane_ref[...],
        precision=lax.Precision.HIGHEST, preferred_element_type=F32,
    )
    return sum(weight * dots[at * 16 : (at + 1) * 16] for at, weight in enumerate(weights))


def own_layers(
    own_ref, low_ref, high_ref, rim_ref, spread_ref, plane_ref, span_ref, tilde_ref, total_ref
):
    cells_at = layers_of(own_ref, low_ref, high_ref)
    for layer in range(SZ):
        tilde_ref[layer] = diffused(cells_at, rim_ref[layer], spread_ref[...], layer)
    total_ref[...] = samples(tilde_ref, plane_ref, [span_row(span_ref, layer) for layer in range(SZ)])


def forcing(
    send_ref, count_ref, own_ref, low_ref, high_ref, tilde_ref, total_ref, rim_low_ref, rim_high_ref, spread_ref,
    pack_ref, plane_ref, span_ref, aim_ref,
    star_ref, out_ref, beside_ref, table_ref, strips_ref,
):
    markers = plane_ref.shape[1]
    group = markers // 2
    cells_at = layers_of(own_ref, low_ref, high_ref)
    halo = [-3, -2, -1, SZ, SZ + 1, SZ + 2]
    for at, layer in enumerate(halo):
        rims = rim_rows(rim_low_ref, layer + SZ - 1) if layer < 0 else rim_rows(rim_high_ref, layer - SZ)
        beside_ref[at] = diffused(cells_at, rims, spread_ref[...], layer)
    total = total_ref[...] + samples(beside_ref, plane_ref, [span_row(span_ref, layer) for layer in halo])
    mine = (lax.broadcasted_iota(jnp.int32, (16, markers), 0) % NB).astype(F32) == aim_ref[3:4, :]
    total = jnp.where(mine, total, 0.0)
    place = lax.broadcasted_iota(jnp.int32, (1, markers), 1) % group
    live = place < count_ref[0]
    rows = []
    for comp in range(3):
        sampled = jnp.sum(total[comp * NB : (comp + 1) * NB], axis=0, keepdims=True)
        force = jnp.where(live, aim_ref[comp : comp + 1, :] - sampled, 0.0)
        rows.append(jnp.broadcast_to(force, (NB, markers)))
    rows.append(jnp.zeros((NB, markers), F32))
    force = jnp.where(mine, jnp.concatenate(rows, axis=0), 0.0)
    pushes = jnp.concatenate([span_row(span_ref, layer) * force for layer in range(SZ)], axis=0)
    spread = lax.dot_general(
        pushes, plane_ref[...], (((1,), (1,)), ((), ())),
        precision=lax.Precision.HIGHEST, preferred_element_type=F32,
    )
    star = tilde_ref[...].reshape(SZ * 16, CELLS) + spread
    planes = []
    cell = lax.broadcasted_iota(jnp.int32, (NB, CELLS), 1)
    for layer in range(SZ):
        rows = star[layer * 16 : (layer + 1) * 16]
        first, second = rows[:NB], rows[NB : 2 * NB]
        inner = jnp.where(cell < CELLS - EDGE, shifted(first, -EDGE), 0.0)
        inner -= jnp.where(cell >= EDGE, shifted(first, EDGE), 0.0)
        inner += jnp.where(cell % EDGE != EDGE - 1, shifted(second, -1), 0.0)
        inner -= jnp.where(cell % EDGE != 0, shifted(second, 1), 0.0)
        planes.append(jnp.concatenate([rows[: 3 * NB], 0.5 * inner], axis=0))
        star_ref[layer] = planes[layer]
    table_ref[...] = jnp.zeros(table_ref.shape, F32)
    strips_ref[...] = pick(jnp.concatenate(planes, axis=0), pack_ref[...]).reshape(SZ, 16, SEG)
    lane = lane_ids(NB)
    comps = [segments(strips_ref, comp * NB) for comp in range(4)]

    def corners(values):
        out = values[0]
        for at in range(1, 4):
            out = jnp.where(lane % 4 == at, values[at], out)
        return out

    def flat_rows(layer, side):
        first, second, inner = (comps[comp](layer, side) for comp in (0, 1, 3))
        edge = pltpu.roll(first if side < 2 else second, 2 * EDGE, axis=1)
        turned = pltpu.roll(first, 1, axis=1)
        patch = corners([inner, turned, turned, pltpu.roll(second, 3, axis=1)])
        return jnp.where(lane < 2 * EDGE, inner, jnp.where(lane < 96, edge, patch))

    def third_rows(layer, side):
        third = comps[2](layer, side)
        patch = jnp.where(lane % 4 == 1, pltpu.roll(comps[1](layer, side), LANES - 1, axis=1), third)
        return jnp.where(lane < 96, third, patch)

    store_table(flat_rows, table_ref, 0, 2)
    store_table(third_rows, table_ref, 1, 2)
    post(send_ref, table_ref, out_ref, 2, out_ref.shape[0] // 2)


def gather_star(got_ref, route_ref, flat_ghost_ref, third_ghost_ref):
    lane = lane_ids(8)
    for block in range(NB):
        for vertex in range(4):
            strip = strip_rows_of(got_ref, route_ref, block, vertex, 0, 2)
            third_strip = strip_rows_of(got_ref, route_ref, block, vertex, 1, 2)
            far = (1 - vertex // 2) * 2 + 1 - vertex % 2
            for sheet in range(2):

                def cell(step, corner, field, index, target):
                    place = route_at(block, vertex, sheet, step)
                    return patch_rows(got_ref, route_ref, place, corner, field, 2, target, index)

                beside = cell(0, far ^ (1 if sheet == 0 else 2), 0, 3 if sheet == 0 else 1, 102 - sheet)
                value = jnp.where(lane < 96, strip, 0.0)
                value = jnp.where(lane == 96, cell(1, far, 0, 0, 96), value)
                across = cell(1, far, 0, 3 if sheet == 0 else 1, 97 + 2 * sheet)
                value = jnp.where(lane == 97 + 2 * sheet, across, value)
                if sheet == 0:
                    deeper = cell(1, far, 1, 1, 98)
                else:
                    deeper = cell(1, far, 0, 2, 100)
                value = jnp.where(lane == 98 + 2 * sheet, deeper, value)
                third = jnp.where(lane == 96, cell(1, far, 1, 0, 96), 0.0)
                third = jnp.where(lane < 96, third_strip, third)
                beyond = far ^ 2 if sheet == 0 else far ^ 1
                last = cell(2, beyond, 0, 1 if sheet == 0 else 3, 101 + sheet)
                value = jnp.where(lane == 101 + sheet, last, value)
                value = jnp.where(lane == 102 - sheet, beside, value)
                row, at = sheet * NB + block, slice(vertex * LANES, (vertex + 1) * LANES)
                for layer in range(SZ):
                    flat_ghost_ref[layer, row : row + 1, at] = value[layer : layer + 1]
                    third_ghost_ref[layer, row : row + 1, at] = third[layer : layer + 1]


def star_unpack(
    route_ref, got_ref, star_ref, spread_ref, place_ref, mask_ref,
    flat_ref, third_ref, up_ref, down_ref, flat_ghost_ref, third_ghost_ref,
):
    gather_star(got_ref, route_ref, flat_ghost_ref, third_ghost_ref)
    flat_placed = pick(flat_ghost_ref[...].reshape(SZ * 8, SEG), spread_ref[...])
    third_placed = pick(third_ghost_ref[...].reshape(SZ * 8, SEG), place_ref[...])
    mask = mask_ref[...] > 0.0
    lane = lax.broadcasted_iota(jnp.int32, (NB, WIDTH), 1)
    row, column = lane // STRIDE - DEPTH, lane % STRIDE - 4
    flats, thirds = [], []
    for layer in range(SZ):
        whole = expand(star_ref[layer])
        first, second = whole[:NB], whole[NB : 2 * NB]
        flat = whole[3 * NB :]
        flat += jnp.where(row == EDGE, -0.5 * shifted(first, STRIDE), 0.0)
        flat += jnp.where(row == -1, 0.5 * shifted(first, -STRIDE), 0.0)
        flat += jnp.where(column == EDGE, -0.5 * shifted(second, 1), 0.0)
        flat += jnp.where(column == -1, 0.5 * shifted(second, -1), 0.0)
        at = layer * 8
        flats.append(merge(second_halves(flat) + flat_placed[at : at + 8], mask))
        thirds.append(second_halves(whole[2 * NB : 3 * NB]) + third_placed[at : at + 8])
        flat_ref[layer] = flats[layer]
        third_ref[layer] = thirds[layer]
    up_ref[0] = (flats[2] + 0.5 * (thirds[3] - thirds[1]))[:NB]
    up_ref[1] = (flats[3] - 0.5 * thirds[2])[:NB]
    up_ref[2] = fold(thirds[3])
    down_ref[0] = fold(thirds[0])
    down_ref[1] = (flats[0] + 0.5 * thirds[1])[:NB]
    down_ref[2] = (flats[1] + 0.5 * (thirds[2] - thirds[0]))[:NB]


def sweep(source, target, first, last, rhs_ref, corr_ref, mask):
    for at in range(first, last):
        here = source[at]
        around = (shifted(here, STRIDE) + shifted(here, -STRIDE)) + (shifted(here, 1) + shifted(here, -1))
        around += source[at - 1] + source[at + 1]
        around -= rhs_ref[at - 1]
        if corr_ref is not None and DEPTH <= at < DEPTH + SZ:
            around += corr_ref[at - DEPTH]
        target[at] = merge(around * (1.0 / 6.0), mask)


def load_layers(work_ref, own_ref, low_ref, high_ref):
    for layer in range(DEPTH):
        work_ref[layer] = unfold(low_ref[layer])
        work_ref[DEPTH + SZ + layer] = unfold(high_ref[layer])
    for layer in range(SZ):
        work_ref[DEPTH + layer] = own_ref[layer]


def three_sweeps(work_ref, other_ref, rhs_ref, corr_ref, mask):
    sweep(work_ref, other_ref, 1, 9, rhs_ref, corr_ref, mask)
    sweep(other_ref, work_ref, 2, 8, rhs_ref, None, mask)
    sweep(work_ref, other_ref, 3, 7, rhs_ref, None, mask)


def send_pressure(send_ref, done_ref, pack_ref, p_ref, out_ref, table_ref, strips_ref):
    p_ref[...] = done_ref[DEPTH : DEPTH + SZ]
    table_ref[...] = jnp.zeros(table_ref.shape, F32)
    strips_ref[...] = pick(p_ref[...].reshape(SZ * 8, WIDTH), pack_ref[...]).reshape(SZ, 8, SEG)
    store_table(segments(strips_ref, 0), table_ref, 0, 1)
    post(send_ref, table_ref, out_ref, 1, out_ref.shape[0])


def first_sweeps(
    send_ref, own_ref, corr_ref, low_ref, high_ref, flat_ref, third_ref, star_low_ref, star_high_ref, mask_ref, pack_ref,
    p_ref, rhs_ref, out_ref, work_ref, other_ref, table_ref, strips_ref,
):
    mask = mask_ref[...] > 0.0
    load_layers(work_ref, own_ref, low_ref, high_ref)

    thirds = [unfold(star_low_ref[2])] + [third_ref[layer] for layer in range(SZ)] + [unfold(star_high_ref[0])]
    for layer in range(SZ):
        rhs_ref[layer + 2] = flat_ref[layer] + 0.5 * (thirds[layer + 2] - thirds[layer])
    rhs_ref[0] = second_halves(star_low_ref[0])
    rhs_ref[1] = second_halves(star_low_ref[1]) + 0.5 * thirds[1]
    rhs_ref[SZ + 2] = second_halves(star_high_ref[1]) - 0.5 * thirds[SZ]
    rhs_ref[SZ + 3] = second_halves(star_high_ref[2])
    three_sweeps(work_ref, other_ref, rhs_ref, corr_ref, mask)
    send_pressure(send_ref, other_ref, pack_ref, p_ref, out_ref, table_ref, strips_ref)


def later_sweeps(
    send_ref, own_ref, corr_ref, low_ref, high_ref, rhs_ref, mask_ref, pack_ref,
    p_ref, out_ref, work_ref, other_ref, table_ref, strips_ref,
):
    load_layers(work_ref, own_ref, low_ref, high_ref)
    three_sweeps(work_ref, other_ref, rhs_ref, corr_ref, mask_ref[...] > 0.0)
    send_pressure(send_ref, other_ref, pack_ref, p_ref, out_ref, table_ref, strips_ref)


def last_sweeps(
    own_ref, corr_ref, low_ref, high_ref, rhs_ref, mask_ref, star_ref, velocity_ref, p_ref, work_ref, other_ref
):
    mask = mask_ref[...] > 0.0
    load_layers(work_ref, own_ref, low_ref, high_ref)
    sweep(work_ref, other_ref, 1, 9, rhs_ref, corr_ref, mask)
    sweep(other_ref, work_ref, 2, 8, rhs_ref, None, mask)
    for layer in range(SZ):
        here = work_ref[DEPTH + layer]
        rows = [
            shifted(here, -STRIDE) - shifted(here, STRIDE),
            shifted(here, -1) - shifted(here, 1),
            work_ref[DEPTH + layer + 1] - work_ref[DEPTH + layer - 1],
            here,
        ]
        flat = compact(jnp.concatenate([row[:NB] for row in rows], axis=0))
        velocity_ref[:, layer, :] = (star_ref[layer] - 0.5 * flat)[: 3 * NB]
        p_ref[:, layer, :] = flat[3 * NB :]


def call(kernel, name, out_shapes, scratch, scalars):
    smem, vmem = pl.BlockSpec(memory_space=pltpu.SMEM), pl.BlockSpec(memory_space=pltpu.VMEM)
    shapes = tuple(jax.ShapeDtypeStruct(shape, F32) for shape in out_shapes)

    def run(*args):
        return pl.pallas_call(
            kernel,
            name=name,
            out_shape=shapes,
            in_specs=[smem if at < scalars else vmem for at in range(len(args))],
            out_specs=tuple(vmem for _ in shapes),
            scratch_shapes=scratch,
            compiler_params=pltpu.CompilerParams(vmem_limit_bytes=24 << 20),
        )(*args)

    return run


def trade(messages, count):
    whole = messages.reshape(count, -1, LANES)
    got = lax.all_to_all(whole, "chord", split_axis=0, concat_axis=0, tiled=True)
    return got.reshape(messages.shape)


def beside(up, down):
    size = lax.axis_size("span")
    low = lax.ppermute(up, "span", [(i, (i + 1) % size) for i in range(size)])
    high = lax.ppermute(down, "span", [(i, (i + size - 1) % size) for i in range(size)])
    return low, high


def local(
    velocity,
    pressure,
    viscosity,
    send_list,
    recv_slot,
    marker_block,
    marker_cells,
    marker_layer,
    marker_frac,
    marker_weights,
    marker_target,
    marker_count,
):
    count, strips = lax.axis_size("chord"), lax.axis_size("span")
    me = lax.axis_index("chord").astype(jnp.int32).reshape(1)
    at = lax.axis_index("span").astype(jnp.int32)
    send = send_list.T
    rim, spread = jnp.asarray(RIM), jnp.asarray(RIM.T)
    pack_flat, pack_ext = jnp.asarray(PACK_FLAT), jnp.asarray(PACK_EXT)
    spread_flat = jnp.asarray(SPREAD)
    place, mask, inside = jnp.asarray(PLACE), jnp.asarray(MASK), jnp.asarray(INSIDE)

    plane, flat = (SZ, 8, WIDTH), (SZ, 16, CELLS)
    tables = lambda fields: pltpu.VMEM((2 * fields * 16, 8, LANES), F32)
    strip_rows = lambda rows: pltpu.VMEM((SZ, rows, SEG), F32)
    layers = pltpu.VMEM((SZ + 2 * DEPTH, 8, WIDTH), F32)

    anywhere = pl.BlockSpec(memory_space=pl.ANY)
    messages = pl.pallas_call(
        first_pack,
        name="first_pack",
        out_shape=jax.ShapeDtypeStruct((2 * count, 8, LANES), F32),
        in_specs=[anywhere] * 5,
        out_specs=pl.BlockSpec(memory_space=pltpu.VMEM),
        scratch_shapes=[
            pltpu.SMEM((2, count), jnp.int32),
            pltpu.VMEM((3 * NB, SZ, CELLS), F32),
            pltpu.VMEM((NB, SZ, CELLS), F32),
            pltpu.VMEM((CELLS, LANES), BF16),
            pltpu.VMEM((CELLS, SEG), BF16),
            tables(2),
            pltpu.SemaphoreType.DMA((5,)),
        ],
        compiler_params=pltpu.CompilerParams(vmem_limit_bytes=60 << 20),
    )(send, velocity.reshape(3 * NB, SZ, CELLS), pressure, rim, pack_flat)
    got = trade(messages, count)
    me, _ = lax.optimization_barrier((me, messages))
    route = pl.pallas_call(
        routes,
        name="routes",
        out_shape=jax.ShapeDtypeStruct((ROUTES,), jnp.int32),
        in_specs=[pl.BlockSpec(memory_space=pltpu.SMEM)] * 3,
        out_specs=pl.BlockSpec(memory_space=pltpu.SMEM),
        scratch_shapes=[pltpu.SMEM((32,), jnp.int32)],
    )(me, send, recv_slot)
    later, eddy, route = lax.optimization_barrier((velocity, viscosity, route))
    cells = jnp.concatenate([later, eddy[None]], axis=0)
    cells = jnp.transpose(cells, (2, 0, 1, 3)).reshape(SZ, 16, CELLS)
    cells_low, cells_high = beside(cells, cells)

    group = marker_block.shape[0] // strips
    groups = jnp.stack([at, (at + strips - 1) % strips])
    weights, spans, aims = call(weigh, "weigh", [(CELLS, 2 * group), (16, 2 * group), (4, 2 * group)], [], 1)(
        groups, marker_block[None], marker_cells, marker_layer[None], marker_frac[None], marker_weights, marker_target
    )

    edge = (DEPTH, NB, WIDTH + 3 * LANES)
    own, corr, rims, up, down = call(
        first_unpack, "first_unpack", [plane, plane, (SZ, 16, LANES), edge, edge], [strip_rows(8), pltpu.VMEM(plane, F32)], 1
    )(route, got, pressure, place)
    low, high = beside(up, down)
    tilde, total = call(own_layers, "own_layers", [flat, (16, 2 * group)], [], 0)(
        cells, cells_low, cells_high, rims, spread, weights, spans
    )
    star, messages = call(
        forcing, "forcing", [flat, (2 * count, 8, LANES)],
        [pltpu.VMEM((6, 16, CELLS), F32), tables(2), strip_rows(16)], 2,
    )(
        send, marker_count, cells, cells_low, cells_high, tilde, total, low, high, spread,
        pack_flat, weights, spans, aims,
    )
    got = trade(messages, count)
    edge = (DEPTH, NB, WIDTH)
    flat_part, third, up, down = call(
        star_unpack, "star_unpack", [plane, plane, edge, edge], [strip_rows(8), strip_rows(8)], 1
    )(route, got, star, spread_flat, place, mask)
    star_low, star_high = beside(up, down)

    p, rhs, messages = call(
        first_sweeps, "first_sweeps", [plane, (SZ + 4, 8, WIDTH), (count, 8, LANES)],
        [layers, layers, tables(1), strip_rows(8)], 1,
    )(send, own, corr, low, high, flat_part, third, star_low, star_high, mask, pack_ext)
    for last in (False, True):
        got = trade(messages, count)
        own, corr, up, down = call(
            later_unpack, "later_unpack", [plane, plane, edge, edge], [strip_rows(8)], 1
        )(route, got, p, place, inside)
        low, high = beside(up, down)
        if not last:
            p, messages = call(
                later_sweeps, "later_sweeps", [plane, (count, 8, LANES)], [layers, layers, tables(1), strip_rows(8)], 1
            )(send, own, corr, low, high, rhs, mask, pack_ext)
    velocity_next, pressure_next = call(
        last_sweeps, "last_sweeps", [(3 * NB, SZ, CELLS), (NB, SZ, CELLS)], [layers, layers], 0
    )(own, corr, low, high, rhs, mask, star)
    return velocity_next.reshape(velocity.shape), pressure_next


RIM = rim_matrix()
PACK_FLAT = pack_matrix(CELLS, lambda i, k: EDGE * i + k)
PACK_EXT = pack_matrix(WIDTH, place_of)
PLACE = place_matrix()
SPREAD = spread_matrix()
MASK = sheet_mask()
INSIDE = block_mask()


def solution(mesh):
    in_specs = (
        P(None, "chord", "span", None),
        P("chord", "span", None),
        P("chord", "span", None),
        P("chord", None),
        P("chord", None),
        P("chord"),
        P(None, "chord"),
        P("chord"),
        P("chord"),
        P(None, "chord"),
        P(None, "chord"),
        P("chord"),
    )
    out_specs = (P(None, "chord", "span", None), P("chord", "span", None))
    return jax.shard_map(local, mesh=mesh, in_specs=in_specs, out_specs=out_specs, check_vma=False)
```

```python
import math

import jax
import jax.numpy as jnp
import ml_dtypes
import numpy as np
from jax import lax
from jax.experimental import pallas as pl
from jax.experimental.pallas import tpu as pltpu
from jax.sharding import PartitionSpec as P

EDGE = 32
CELLS = EDGE * EDGE
NB = 4
SZ = 4
REACH = 3
DEPTH = 4
STRIDE = 40
WIDTH = 1664
LANES = 128
SEG = 4 * LANES
PATCH = ((0, 0), (0, 1), (1, 0), (0, 2), (1, 1), (2, 0))
F32 = jnp.float32
BF16 = jnp.bfloat16


def place_of(i, k):
    return STRIDE * (i + DEPTH) + k + 4


def edge_cell(side, depth, x):
    return [(depth, x), (EDGE - 1 - depth, x), (x, depth), (x, EDGE - 1 - depth)][side]


def ghost_cell(side, depth, x):
    return [(-1 - depth, x), (EDGE + depth, x), (x, -1 - depth), (x, EDGE + depth)][side]


def corner_cell(corner, i, k):
    return i if corner // 2 == 0 else EDGE - 1 - i, k if corner % 2 == 0 else EDGE - 1 - k


def vertex_cell(vertex, i=0, k=0):
    return -1 - i if vertex // 2 == 0 else EDGE + i, -1 - k if vertex % 2 == 0 else EDGE + k


def pack_matrix(rows, where):
    table = np.zeros((rows, SEG + LANES), np.float32)
    for side in range(4):
        for depth in range(DEPTH):
            for x in range(EDGE):
                table[where(*edge_cell(side, depth, x)), side * LANES + depth * EDGE + x] = 1
    for corner in range(4):
        for at, cell in enumerate(PATCH):
            table[where(*corner_cell(corner, *cell)), SEG + corner * 8 + at] = 1
    return table.astype(ml_dtypes.bfloat16)


def pack_rhs_matrix():
    table = np.zeros((CELLS, SEG), np.float32)
    for side in range(4):
        for depth in range(DEPTH - 1):
            for x in range(EDGE):
                i, k = edge_cell(side, depth, x)
                table[EDGE * i + k, side * LANES + depth * EDGE + x] = 1
        for corner in range(4):
            for at in range(4):
                i, k = corner_cell(corner, at // 2, at % 2)
                table[EDGE * i + k, side * LANES + 96 + corner * 4 + at] = 1
    return table.astype(ml_dtypes.bfloat16)


def place_matrix():
    table = np.zeros((SEG + LANES, WIDTH), np.float32)
    for side in range(4):
        for depth in range(DEPTH):
            for x in range(EDGE):
                table[side * LANES + depth * EDGE + x, place_of(*ghost_cell(side, depth, x))] = 1
    for vertex in range(4):
        for at, cell in enumerate(PATCH):
            table[SEG + vertex * 16 + at, place_of(*vertex_cell(vertex, *cell))] = 1
    return table.astype(ml_dtypes.bfloat16)


def place_rhs_matrix():
    table = np.zeros((SEG, WIDTH), np.float32)
    for side in range(4):
        for depth in range(DEPTH - 1):
            for x in range(EDGE):
                table[side * LANES + depth * EDGE + x, place_of(*ghost_cell(side, depth, x))] = 1
    for vertex in range(4):
        for at in range(3):
            table[vertex * LANES + 96 + at, place_of(*vertex_cell(vertex, at // 2, at % 2))] = 1
    return table.astype(ml_dtypes.bfloat16)


def across_matrix():
    table = np.zeros((LANES, CELLS), np.float32)
    for side in range(4):
        for x in range(EDGE):
            i, k = edge_cell(side, 0, x)
            table[side * EDGE + x, i * EDGE + k] = 0.5 if side % 2 else -0.5
    return table.astype(ml_dtypes.bfloat16)


def fan_codes():
    codes = np.zeros((8, WIDTH), np.float32)
    for vertex in range(4):
        to_i, to_k = 1 + (1 - vertex // 2), 3 + (1 - vertex % 2)
        codes[:NB, place_of(*vertex_cell(vertex))] = to_i
        codes[:NB, place_of(*vertex_cell(vertex, 0, 1))] = to_i + 4
        codes[NB:, place_of(*vertex_cell(vertex))] = to_k
        codes[NB:, place_of(*vertex_cell(vertex, 1, 0))] = to_k + 4
    return codes


def rim_matrix():
    table = np.zeros((CELLS, LANES), np.float32)
    for side in range(4):
        for x in range(EDGE):
            i, k = edge_cell(side, 0, x)
            table[i * EDGE + k, side * EDGE + x] = 1
    return table.astype(ml_dtypes.bfloat16)


def sheet_mask():
    mask = np.zeros((8, WIDTH), np.float32)
    for i in range(-DEPTH, EDGE + DEPTH):
        for k in range(-DEPTH, EDGE + DEPTH):
            inside_i, inside_k = 0 <= i < EDGE, 0 <= k < EDGE
            if inside_i and not inside_k:
                mask[:4, place_of(i, k)] = 1
            if inside_k and not inside_i:
                mask[4:, place_of(i, k)] = 1
    return mask


def block_mask():
    mask = np.zeros((8, WIDTH), np.float32)
    for i in range(EDGE):
        mask[:, place_of(i, 0) : place_of(i, 0) + EDGE] = 1
    return mask


def vertex_place(vertex):
    return place_of(*vertex_cell(vertex))


def pick(x, table):
    high = x.astype(BF16)
    rest = x - high.astype(F32)
    middle = rest.astype(BF16)
    low = (rest - middle.astype(F32)).astype(BF16)
    parts = jnp.dot(jnp.concatenate([high, middle, low], axis=0), table, preferred_element_type=F32)
    rows = x.shape[0]
    return (parts[:rows] + parts[rows : 2 * rows]) + parts[2 * rows :]


def shifted(x, lanes):
    return pltpu.roll(x, lanes % x.shape[1], axis=1)


def lane_ids(rows):
    return lax.broadcasted_iota(jnp.int32, (rows, LANES), 1)


def remap(x, width, pieces):
    rows = x.shape[0]
    lane = lane_ids(rows)
    out = []
    for tile in range(width // LANES):
        acc = jnp.zeros((rows, LANES), F32)
        base = tile * LANES
        for src, dst in pieces:
            first, last = max(dst, base), min(dst + EDGE, base + LANES)
            while first < last:
                at = src + first - dst
                column = at // LANES
                stop = min(last, first + (column + 1) * LANES - at)
                value = x[:, column * LANES : (column + 1) * LANES]
                turn = (first - base - at % LANES) % LANES
                if turn:
                    value = pltpu.roll(value, turn, axis=1)
                acc = jnp.where((lane >= first - base) & (lane < stop - base), value, acc)
                first = stop
        out.append(acc)
    return jnp.concatenate(out, axis=1)


def expand(x):
    return remap(x, WIDTH, [(EDGE * i, place_of(i, 0)) for i in range(EDGE)])


def compact(x):
    return remap(x, CELLS, [(place_of(i, 0), EDGE * i) for i in range(EDGE)])


def post(send_ref, out_ref, count, parts):
    units = len(parts)

    def one(target, carry):
        edges = [jnp.maximum(send_ref[slot, target], 0) for slot in range(2)]
        for unit, (table, slot, offset) in enumerate(parts):
            out_ref[target * units + unit] = table[offset if slot is None else offset + edges[slot]]
        return carry

    lax.fori_loop(0, count, one, 0, unroll=4)


def store_strips(strips, table_ref, corner_ref):
    lane = lane_ids(SZ)
    corners = jnp.zeros((SZ, LANES), F32)
    for block in range(NB):
        rows = strips[block * SZ : (block + 1) * SZ]
        for side in range(4):
            table_ref[block * 4 + side] = rows[:, side * LANES : (side + 1) * LANES]
        patch = rows[:, SEG:]
        patch = pltpu.roll(patch, EDGE * block, axis=1) if block else patch
        corners = jnp.where(lane // EDGE == block, patch, corners)
    corner_ref[0] = corners


def store_rhs_strips(strips, table_ref):
    lane = lane_ids(SZ)
    for side in range(4):
        parts = [strips[block * SZ : (block + 1) * SZ, side * LANES : (side + 1) * LANES] for block in range(NB)]
        for slot in range(2):
            patch = jnp.where(lane < 112, parts[2 * slot], pltpu.roll(parts[2 * slot + 1], 16, axis=1))
            for block in range(NB):
                table_ref[slot * 16 + block * 4 + side] = jnp.where(lane < 96, parts[block], patch)


def first_pack(
    send_any, velocity_any, p_any, rim_any, out_ref, send_ref, velocity_ref, p_ref, rim_ref, table_ref, done_ref
):
    pairs = ((velocity_any, velocity_ref), (rim_any, rim_ref), (p_any, p_ref), (send_any, send_ref))
    copies = [pltpu.make_async_copy(*pair, done_ref.at[at]) for at, pair in enumerate(pairs)]
    for copy in copies:
        copy.start()
    lane = lane_ids(SZ)
    for copy in copies:
        copy.wait()
    rows = [velocity_ref[...].reshape(3 * NB * SZ, CELLS), p_ref[...].reshape(NB * SZ, CELLS)]
    rims = pick(jnp.concatenate(rows, axis=0), rim_ref[...])
    for block in range(NB):
        for side in range(4):
            value = jnp.zeros((SZ, LANES), F32)
            for comp in range(4):
                first = (comp * NB + block) * SZ
                part = rims[first : first + SZ]
                turn = EDGE * (comp - side) % LANES
                if turn:
                    part = pltpu.roll(part, turn, axis=1)
                value = jnp.where(lane // EDGE == comp, part, value)
            table_ref[block * 4 + side] = value
    post(send_ref, out_ref, out_ref.shape[0] // 2, [(table_ref, 0, 0), (table_ref, 1, 0)])


def routes(me_ref, send_ref, recv_ref, out_ref, near_ref):
    me, count = me_ref[0], send_ref.shape[1]
    for edge in range(16):
        block, side = edge // 4, edge % 4
        entry = recv_ref[block, side]
        source, slot = entry // 2, entry % 2
        out_ref[2 * edge], out_ref[2 * edge + 1] = source, slot
        back = lax.rem(2 * me - source + count, count)
        near_ref[edge] = send_ref[slot, back] // 4
        near_ref[16 + edge] = lax.rem(source - me + count, count)
    for block in range(NB):
        for vertex in range(4):
            i_side, k_side = vertex // 2, 2 + vertex % 2
            for sheet, (side, then) in enumerate(((i_side, k_side), (k_side, i_side))):
                at, offset = block, 0
                for step, across in enumerate((side, then, side ^ 1, then ^ 1)):
                    edge = at * 4 + across
                    at, offset = near_ref[edge], offset + near_ref[16 + edge]
                    place = route_at(block, vertex, sheet, step)
                    out_ref[place] = lax.rem(me + offset, count)
                    out_ref[place + 1] = at


def route_at(block, vertex, sheet, step):
    return 32 + (((block * 4 + vertex) * 2 + sheet) * 4 + step) * 2


ROUTES = 32 + 32 * 8


def strip_of(got_ref, route_ref, block, side, unit, units):
    edge = block * 4 + side
    return got_ref[route_ref[2 * edge] * units + unit + route_ref[2 * edge + 1]]


def turned(rows, target, lane):
    return pltpu.roll(rows, lax.rem(target + LANES - lane, LANES), axis=1)


def gather_ghosts(got_ref, route_ref, ghost_ref, fan_ref, units, old_ref):
    lane = lane_ids(SZ)
    for block in range(NB):
        for side in range(4):
            strip = strip_of(got_ref, route_ref, block, side, 0, units)
            for sheet in range(2):
                ghost_ref[:, sheet * NB + block, side * LANES : (side + 1) * LANES] = strip
        for sheet in range(2):
            row = sheet * NB + block
            value = jnp.zeros((SZ, LANES), F32) if old_ref is None else old_ref[:, row, :]
            for vertex in range(4):
                far = (1 - vertex // 2) * 2 + 1 - vertex % 2
                beyond = far ^ 2 if sheet == 0 else far ^ 1
                first = vertex * 16

                def cells(step, corner, target, low, high, value):
                    place = route_at(block, vertex, sheet, step)
                    rows = got_ref[route_ref[place] * units + 2]
                    rows = turned(rows, target, route_ref[place + 1] * EDGE + corner * 8)
                    return jnp.where((lane >= low) & (lane < high), rows, value)

                value = cells(1, far, first, first, first + 6, value)
                value = cells(2, beyond, first + 6, first + 6, first + 9, value)
                value = cells(3, vertex, first + 9, first + 9, first + 10, value)
                if old_ref is None:
                    place = route_at(block, vertex, sheet, 2)
                    at = route_ref[place + 1]
                    rows = got_ref[route_ref[place] * units + 3 + at // 2]
                    rows = turned(rows, first + 10, 96 + (at % 2) * 16 + beyond * 4)
                    value = jnp.where(lane == first + 10, rows, value)
            ghost_ref[:, row, SEG:] = value
            fan_ref[:, row, :] = value


def gather_rhs(got_ref, route_ref, ghost_ref, units):
    lane = lane_ids(SZ)
    for block in range(NB):
        for vertex in range(4):
            strip = strip_of(got_ref, route_ref, block, vertex, 3, units)
            far = (1 - vertex // 2) * 2 + 1 - vertex % 2
            for sheet in range(2):
                place = route_at(block, vertex, sheet, 1)
                at = route_ref[place + 1]
                rows = got_ref[route_ref[place] * units + 3 + at // 2]
                rows = turned(rows, 96, (96 + (at % 2) * 16 + far * 4))
                value = jnp.where(lane < 96, strip, jnp.where(lane < 99, rows, 0.0))
                ghost_ref[:, sheet * NB + block, vertex * LANES : (vertex + 1) * LANES] = value


def moved(tiles, value, lane_from, place):
    tile, at = place // LANES, place % LANES
    turn = (at - lane_from) % LANES
    value = pltpu.roll(value, turn, axis=1) if turn else value
    tiles[tile] = jnp.where(lane_ids(value.shape[0]) == at, value, tiles[tile])


def tiles_of(x):
    return [x[:, at : at + LANES] for at in range(0, WIDTH, LANES)]


def fold(ext):
    last = [ext[:NB, WIDTH - LANES : WIDTH]]
    for vertex in range(4):
        place = vertex_place(vertex)
        tile = place // LANES * LANES
        moved(last, ext[NB:, tile : tile + LANES], place % LANES, 112 + vertex)
    return jnp.concatenate([ext[:NB, : WIDTH - LANES], last[0]], axis=1)


def unfold(rows):
    tiles = tiles_of(rows)
    last = tiles[-1]
    for vertex in range(4):
        moved(tiles, last, 112 + vertex, vertex_place(vertex))
    return jnp.concatenate([rows[:, :WIDTH], jnp.concatenate(tiles, axis=1)], axis=0)


def both_sheets(rows, corners):
    tiles = tiles_of(rows)
    if corners:
        segment = rows[:, WIDTH + LANES : WIDTH + 2 * LANES]
        for vertex in range(4):
            for at in range(3):
                moved(tiles, segment, vertex * 16 + at, place_of(*vertex_cell(vertex, *PATCH[at])))
    return jnp.concatenate([rows[:, :WIDTH], jnp.concatenate(tiles, axis=1)], axis=0)


def corner_tiles():
    cells = [vertex_cell(vertex, *cell) for vertex in range(4) for cell in PATCH[:3]]
    return sorted({place_of(*cell) // LANES for cell in cells})


def third_cells(fan):
    tiles = {tile: jnp.zeros((8, LANES), F32) for tile in corner_tiles()}
    for vertex in range(4):
        moved(tiles, fan, vertex * 16 + 6, vertex_place(vertex))
        moved(tiles, fan, vertex * 16 + 7, place_of(*vertex_cell(vertex, 0, 1)))
        moved(tiles, fan, vertex * 16 + 8, place_of(*vertex_cell(vertex, 1, 0)))
    return tiles


def third_sums(fan):
    total = (fan + shifted(fan, -1)) + (shifted(fan, -2) - shifted(fan, -3))
    tiles = {tile: jnp.zeros((8, LANES), F32) for tile in corner_tiles()}
    for vertex in range(4):
        moved(tiles, total, vertex * 16 + 7, vertex_place(vertex))
    return tiles


def merge(x, mask):
    return jnp.where(mask, pltpu.roll(x, NB, axis=0), x)


def second_halves(x):
    return jnp.concatenate([x, x], axis=0)


def first_unpack(route_ref, got_ref, p_ref, rim_ref, up_ref, down_ref):
    lane = lane_ids(SZ)
    for block in range(NB):
        strips = [strip_of(got_ref, route_ref, block, side, 0, 2) for side in range(4)]
        for comp in range(4):
            value = jnp.zeros((SZ, LANES), F32)
            for side in range(4):
                turn = EDGE * (side - comp) % LANES
                part = pltpu.roll(strips[side], turn, axis=1) if turn else strips[side]
                value = jnp.where(lane // EDGE == side, part, value)
            rim_ref[:, comp * NB + block, :] = value
    for layer in range(REACH):
        for comp in range(3):
            at = (layer * 3 + comp) * LANES
            up_ref[:, at : at + LANES] = rim_ref[layer + 1, comp * NB : (comp + 1) * NB, :]
            down_ref[:, at : at + LANES] = rim_ref[layer, comp * NB : (comp + 1) * NB, :]
    up_ref[:, RIMS:] = p_ref[:, SZ - 1, :]
    down_ref[:, RIMS:] = p_ref[:, 0, :]


RIMS = 3 * REACH * LANES


def send_planes(ext, fan, layer, up_ref, down_ref):
    for ref in (up_ref, down_ref):
        ref[layer, :, :WIDTH] = ext[:NB]
        ref[layer, :, WIDTH : WIDTH + LANES] = fan[:NB]
        ref[layer, :, WIDTH + LANES :] = fan[NB:]


def middle_unpack(
    route_ref, got_ref, p_ref, rhs_ref, place_ref, place_rhs_ref,
    own_ref, fan_ref, div_ref, up_ref, down_ref, ghost_ref, rhs_ghost_ref, block_ref,
):
    gather_ghosts(got_ref, route_ref, ghost_ref, fan_ref, 5, None)
    gather_rhs(got_ref, route_ref, rhs_ghost_ref, 5)
    placed = pick(ghost_ref[...].reshape(SZ * 8, SEG + LANES), place_ref[...])
    placed_rhs = pick(rhs_ghost_ref[...].reshape(SZ * 8, SEG), place_rhs_ref[...])
    for which, ref in enumerate((p_ref, rhs_ref)):
        whole = expand(ref[...].reshape(NB * SZ, CELLS))
        for block in range(NB):
            for sheet in range(2):
                block_ref[which, :, sheet * NB + block, :] = whole[block * SZ : (block + 1) * SZ]
    for layer in range(SZ):
        ext = block_ref[0, layer] + placed[layer * 8 : (layer + 1) * 8]
        own_ref[layer] = ext
        send_planes(ext, fan_ref[layer], layer, up_ref, down_ref)
        ext = block_ref[1, layer] + placed_rhs[layer * 8 : (layer + 1) * 8]
        div_ref[layer] = ext
        if layer >= 1:
            up_ref[SZ + layer - 1, :, :WIDTH] = fold(ext)
        if layer < SZ - 1:
            down_ref[SZ + layer, :, :WIDTH] = fold(ext)


def last_unpack(
    route_ref, got_ref, p_ref, old_ref, place_ref, block_ref, own_ref, fan_ref, up_ref, down_ref, ghost_ref
):
    gather_ghosts(got_ref, route_ref, ghost_ref, fan_ref, 3, old_ref)
    placed = pick(ghost_ref[...].reshape(SZ * 8, SEG + LANES), place_ref[...])
    for layer in range(SZ):
        ext = jnp.where(block_ref[...] > 0.0, p_ref[layer], 0.0) + placed[layer * 8 : (layer + 1) * 8]
        own_ref[layer] = ext
        send_planes(ext, fan_ref[layer], layer, up_ref, down_ref)


def rim_rows(ref, layer):
    rows = [ref[:, (3 * layer + comp) * LANES : (3 * layer + comp + 1) * LANES] for comp in range(3)]
    return jnp.concatenate(rows + [jnp.zeros((NB, LANES), F32)], axis=0)


def halves(x):
    high = x.astype(BF16)
    return high, (x - high.astype(F32)).astype(BF16)


def product(x, high, low, contract):
    rows = x.shape[0]
    dims = (((1,), (contract,)), ((), ()))
    parts = halves(x)
    both = lax.dot_general(jnp.concatenate(parts, axis=0), high, dims, preferred_element_type=F32)
    return (both[:rows] + both[rows:]) + lax.dot_general(parts[0], low, dims, preferred_element_type=F32)


def weigh(
    at_ref, block_ref, cells_ref, layer_ref, fraction_ref, weight_ref, target_ref, high_ref, low_ref, span_ref, aim_ref
):
    group = high_ref.shape[1] // 2
    along = lax.broadcasted_iota(jnp.int32, (EDGE, group), 0)
    for which in range(2):
        lanes = pl.ds(pl.multiple_of(at_ref[which] * group, group), group)
        here = slice(which * group, (which + 1) * group)
        corner = cells_ref[0:1, lanes]
        row_i, row_k = corner // EDGE, corner % EDGE
        weight = weight_ref[:, lanes]
        lines = []
        for a in range(4):
            line = jnp.zeros((EDGE, group), F32)
            for b in range(4):
                line = jnp.where(along == row_k + b, weight[4 * a + b : 4 * a + b + 1], line)
            lines.append(line)
        for i in range(EDGE):
            value = jnp.zeros((EDGE, group), F32)
            for a in range(4):
                value = jnp.where(row_i + a == i, lines[a], value)
            high, low = halves(value)
            high_ref[i * EDGE : (i + 1) * EDGE, here] = high
            low_ref[i * EDGE : (i + 1) * EDGE, here] = low
        start = layer_ref[:, lanes] - (at_ref[which] + which) * SZ
        fraction = fraction_ref[:, lanes]
        phi = [0.25 * (1.0 + jnp.cos(0.5 * math.pi * distance)) for distance in
               (1.0 + fraction, fraction, 1.0 - fraction, 2.0 - fraction)]
        for at in range(SZ + 2 * REACH):
            value = jnp.zeros((1, group), F32)
            for a in range(4):
                value = jnp.where(start + a == at - REACH, phi[a], value)
            span_ref[at : at + 1, here] = value
        aim_ref[0:3, here] = target_ref[:, lanes]
        aim_ref[3:4, here] = block_ref[:, lanes].astype(F32)


def diffused(cells_at, rims, spread, layer):
    cell = lax.broadcasted_iota(jnp.int32, (16, CELLS), 1)
    here = cells_at(layer)
    around = jnp.where(cell >= EDGE, shifted(here, EDGE), 0.0)
    around += jnp.where(cell < CELLS - EDGE, shifted(here, -EDGE), 0.0)
    around += jnp.where(cell % EDGE != 0, shifted(here, 1), 0.0)
    around += jnp.where(cell % EDGE != EDGE - 1, shifted(here, -1), 0.0)
    around += pick(rims, spread)
    around += cells_at(layer - 1) + cells_at(layer + 1)
    eddy = second_halves(second_halves(here[3 * NB :]))
    return here + eddy * (around - 6.0 * here)


def span_row(span_ref, layer):
    return span_ref[layer + REACH : layer + REACH + 1, :]


def layers_of(own_ref, low_ref, high_ref):
    def at(layer):
        if layer < 0:
            return low_ref[layer + SZ]
        return own_ref[layer] if layer < SZ else high_ref[layer - SZ]

    return at


def samples(tilde_ref, plane_high_ref, plane_low_ref, weights):
    dots = product(tilde_ref[...].reshape(len(weights) * 16, CELLS), plane_high_ref[...], plane_low_ref[...], 0)
    return sum(weight * dots[at * 16 : (at + 1) * 16] for at, weight in enumerate(weights))


def own_layers(
    own_ref, low_ref, high_ref, rim_ref, spread_ref, plane_high_ref, plane_low_ref, span_ref, tilde_ref, total_ref
):
    cells_at = layers_of(own_ref, low_ref, high_ref)
    for layer in range(SZ):
        tilde_ref[layer] = diffused(cells_at, rim_ref[layer], spread_ref[...], layer)
    total_ref[...] = samples(tilde_ref, plane_high_ref, plane_low_ref, [span_row(span_ref, layer) for layer in range(SZ)])


def forcing(
    send_ref, count_ref, own_ref, low_ref, high_ref, tilde_ref, total_ref, rim_low_ref, rim_high_ref, spread_ref,
    edge_ref, plane_high_ref, plane_low_ref, span_ref, aim_ref, star_ref, out_ref, up_ref, down_ref, beside_ref, table_ref,
):
    markers = plane_high_ref.shape[1]
    group = markers // 2
    cells_at = layers_of(own_ref, low_ref, high_ref)
    halo = [-3, -2, -1, SZ, SZ + 1, SZ + 2]
    for at, layer in enumerate(halo):
        rims = rim_rows(rim_low_ref, layer + SZ - 1) if layer < 0 else rim_rows(rim_high_ref, layer - SZ)
        beside_ref[at] = diffused(cells_at, rims, spread_ref[...], layer)
    total = total_ref[...] + samples(beside_ref, plane_high_ref, plane_low_ref, [span_row(span_ref, layer) for layer in halo])
    mine = (lax.broadcasted_iota(jnp.int32, (16, markers), 0) % NB).astype(F32) == aim_ref[3:4, :]
    total = jnp.where(mine, total, 0.0)
    place = lax.broadcasted_iota(jnp.int32, (1, markers), 1) % group
    live = place < count_ref[0]
    rows = []
    for comp in range(3):
        sampled = jnp.sum(total[comp * NB : (comp + 1) * NB], axis=0, keepdims=True)
        force = jnp.where(live, aim_ref[comp : comp + 1, :] - sampled, 0.0)
        rows.append(jnp.broadcast_to(force, (NB, markers)))
    rows.append(jnp.zeros((NB, markers), F32))
    force = jnp.where(mine, jnp.concatenate(rows, axis=0), 0.0)
    pushes = jnp.concatenate([span_row(span_ref, layer) * force for layer in range(SZ)], axis=0)
    spread = product(pushes, plane_high_ref[...], plane_low_ref[...], 1)
    star = tilde_ref[...].reshape(SZ * 16, CELLS) + spread
    star_ref[...] = star.reshape(SZ, 16, CELLS)
    up_ref[...] = star_ref[SZ - 1, 2 * NB : 3 * NB, :]
    down_ref[...] = star_ref[0, 2 * NB : 3 * NB, :]
    rims = pick(star, edge_ref[...])
    lane = lane_ids(NB)
    for side in range(4):
        value = jnp.zeros((NB, LANES), F32)
        for layer in range(SZ):
            row = layer * 16 + side // 2 * NB
            part = rims[row : row + NB]
            turn = EDGE * (layer - side) % LANES
            if turn:
                part = pltpu.roll(part, turn, axis=1)
            value = jnp.where(lane // EDGE == layer, part, value)
        for block in range(NB):
            table_ref[block * 4 + side] = value[block : block + 1]

    def one(target, carry):
        for slot in range(2):
            out_ref[target, slot : slot + 1, :] = table_ref[jnp.maximum(send_ref[slot, target], 0)]
        return carry

    lax.fori_loop(0, out_ref.shape[0], one, 0, unroll=4)


def half_step(star_ref, p_ref, low_ref, high_ref, rim_ref, spread_ref, out_ref):
    cell = lax.broadcasted_iota(jnp.int32, (NB, CELLS), 1)
    left, right = cell >= EDGE, cell < CELLS - EDGE
    front, back = cell % EDGE != 0, cell % EDGE != EDGE - 1
    rims = pick(jnp.concatenate([rim_ref[layer, 3 * NB :, :] for layer in range(SZ)], axis=0), spread_ref[...])

    def pressure_at(layer):
        if layer < 0:
            return low_ref[:, RIMS:]
        return p_ref[:, layer, :] if layer < SZ else high_ref[:, RIMS:]

    planes = [pressure_at(layer) for layer in range(-1, SZ + 1)]
    for layer in range(SZ):
        rows = star_ref[layer]
        first, second = rows[:NB], rows[NB : 2 * NB]
        flat = jnp.where(right, shifted(first, -EDGE), 0.0) - jnp.where(left, shifted(first, EDGE), 0.0)
        flat += jnp.where(back, shifted(second, -1), 0.0) - jnp.where(front, shifted(second, 1), 0.0)
        if layer < SZ - 1:
            flat += star_ref[layer + 1, 2 * NB : 3 * NB, :]
        if layer > 0:
            flat -= star_ref[layer - 1, 2 * NB : 3 * NB, :]
        out_ref[layer, :NB] = 0.5 * flat
        here = planes[layer + 1]
        around = jnp.where(left, shifted(here, EDGE), 0.0) + jnp.where(right, shifted(here, -EDGE), 0.0)
        around += jnp.where(front, shifted(here, 1), 0.0) + jnp.where(back, shifted(here, -1), 0.0)
        around += rims[layer * NB : (layer + 1) * NB] + (planes[layer] + planes[layer + 2])
        out_ref[layer, NB:] = around


def first_step(
    route_ref, send_ref, got_ref, star_ref, pressure_ref, p_low_ref, p_high_ref, rim_ref, spread_ref,
    low_ref, high_ref, across_ref, pack_ref, pack_rhs_ref,
    p_ref, rhs_ref, out_ref, half_ref, near_ref, table_ref, corner_ref, rhs_table_ref,
):
    half_step(star_ref, pressure_ref, p_low_ref, p_high_ref, rim_ref, spread_ref, half_ref)
    lane = lane_ids(NB)
    for side in range(4):
        for block in range(NB):
            edge = block * 4 + side
            rows = got_ref[route_ref[2 * edge]]
            near_ref[side, block : block + 1, :] = jnp.where(route_ref[2 * edge + 1] == 1, rows[1:2], rows[0:1])
    beyond = []
    for layer in range(SZ):
        value = jnp.zeros((NB, LANES), F32)
        for side in range(4):
            turn = EDGE * (side - layer) % LANES
            part = pltpu.roll(near_ref[side], turn, axis=1) if turn else near_ref[side]
            value = jnp.where(lane // EDGE == side, part, value)
        beyond.append(value)
    across = pick(jnp.concatenate(beyond, axis=0), across_ref[...])
    for layer in range(SZ):
        rhs = half_ref[layer, :NB, :] + across[layer * NB : (layer + 1) * NB]
        if layer == 0:
            rhs -= 0.5 * low_ref[...]
        if layer == SZ - 1:
            rhs += 0.5 * high_ref[...]
        rhs_ref[:, layer, :] = rhs
        p_ref[:, layer, :] = (half_ref[layer, NB:, :] - rhs) * (1.0 / 6.0)
    store_strips(pick(p_ref[...].reshape(NB * SZ, CELLS), pack_ref[...]), table_ref, corner_ref)
    store_rhs_strips(pick(rhs_ref[...].reshape(NB * SZ, CELLS), pack_rhs_ref[...]), rhs_table_ref)
    post(
        send_ref, out_ref, out_ref.shape[0] // 5,
        [(table_ref, 0, 0), (table_ref, 1, 0), (corner_ref, None, 0), (rhs_table_ref, 0, 0), (rhs_table_ref, 1, 16)],
    )


def sweep(source, target, step, rhs_ref, mask, codes, thirds):
    layers = SZ + 2 * DEPTH
    for at in range(step, layers - step):
        here = source[at]
        sides = [shifted(here, STRIDE), shifted(here, -STRIDE), shifted(here, 1), shifted(here, -1)]
        if at - DEPTH in thirds:
            for side in range(4):
                tiles = tiles_of(sides[side])
                for tile, cells in thirds[at - DEPTH].items():
                    code = codes[tile]
                    found = code == side + 1
                    if step == 1:
                        found = found | (code == side + 5)
                    tiles[tile] = jnp.where(found, cells, tiles[tile])
                sides[side] = jnp.concatenate(tiles, axis=1)
        around = (sides[0] + sides[1]) + (sides[2] + sides[3])
        around += source[at - 1] + source[at + 1]
        around -= rhs_ref[at - 1]
        target[at] = merge(around * (1.0 / 6.0), mask)


def load_layers(work_ref, own_ref, low_ref, high_ref):
    for layer in range(SZ):
        work_ref[layer] = both_sheets(low_ref[layer], layer >= 2)
        work_ref[DEPTH + layer] = own_ref[layer]
        work_ref[DEPTH + SZ + layer] = both_sheets(high_ref[layer], layer < 2)


def beside_segments(ref, layer):
    return jnp.concatenate([ref[layer, :, WIDTH : WIDTH + LANES], ref[layer, :, WIDTH + LANES :]], axis=0)


def sweeps(work_ref, other_ref, own_ref, fan_ref, low_ref, high_ref, rhs_ref, mask, codes, steps):
    load_layers(work_ref, own_ref, low_ref, high_ref)
    codes = tiles_of(codes)
    thirds = {layer: third_cells(fan_ref[layer]) for layer in range(SZ)}
    thirds[-1] = third_cells(beside_segments(low_ref, SZ - 1))
    thirds[SZ] = third_cells(beside_segments(high_ref, 0))
    later = {}
    for layer in range(SZ):
        later[layer] = {}
        for tile, total in third_sums(fan_ref[layer]).items():
            around = total + own_ref[layer, :, tile * LANES : (tile + 1) * LANES]
            later[layer][tile] = (around + (thirds[layer - 1][tile] + thirds[layer + 1][tile])) * (1.0 / 6.0)
    refs = (work_ref, other_ref)
    for step in range(1, steps + 1):
        given = thirds if step == 1 else later if step == 2 else {}
        sweep(refs[(step + 1) % 2], refs[step % 2], step, rhs_ref, mask, codes, given)
    return refs[steps % 2]


def middle_sweeps(
    send_ref, own_ref, fan_ref, low_ref, high_ref, div_ref, mask_ref, codes_ref, pack_ref,
    p_ref, rhs_ref, out_ref, work_ref, other_ref, rows_ref, table_ref, corner_ref,
):
    for layer in range(REACH):
        rhs_ref[layer] = unfold(low_ref[SZ + layer])
        rhs_ref[REACH + SZ + layer] = unfold(high_ref[SZ + layer])
    for layer in range(SZ):
        rhs_ref[REACH + layer] = div_ref[layer]
    done = sweeps(
        work_ref, other_ref, own_ref, fan_ref, low_ref, high_ref, rhs_ref, mask_ref[...] > 0.0, codes_ref[...], 4
    )
    for layer in range(SZ):
        here = done[DEPTH + layer]
        p_ref[layer] = here
        rows_ref[:, layer, :] = here[:NB]
    store_strips(pick(rows_ref[...].reshape(NB * SZ, WIDTH), pack_ref[...]), table_ref, corner_ref)
    post(
        send_ref, out_ref, out_ref.shape[0] // 3, [(table_ref, 0, 0), (table_ref, 1, 0), (corner_ref, None, 0)]
    )


def last_sweeps(
    own_ref, fan_ref, low_ref, high_ref, rhs_ref, mask_ref, codes_ref, star_ref, velocity_ref, p_ref, work_ref, other_ref
):
    done = sweeps(
        work_ref, other_ref, own_ref, fan_ref, low_ref, high_ref, rhs_ref, mask_ref[...] > 0.0, codes_ref[...], 3
    )
    for layer in range(SZ):
        here = done[DEPTH + layer]
        rows = [
            shifted(here, -STRIDE) - shifted(here, STRIDE),
            shifted(here, -1) - shifted(here, 1),
            done[DEPTH + layer + 1] - done[DEPTH + layer - 1],
            here,
        ]
        flat = compact(jnp.concatenate([row[:NB] for row in rows], axis=0))
        velocity_ref[:, layer, :] = (star_ref[layer] - 0.5 * flat)[: 3 * NB]
        p_ref[:, layer, :] = flat[3 * NB :]


def call(kernel, name, out_shapes, scratch, scalars, types=None):
    smem, vmem = pl.BlockSpec(memory_space=pltpu.SMEM), pl.BlockSpec(memory_space=pltpu.VMEM)
    types = types or (F32,) * len(out_shapes)
    shapes = tuple(jax.ShapeDtypeStruct(shape, held) for shape, held in zip(out_shapes, types))

    def run(*args):
        return pl.pallas_call(
            kernel,
            name=name,
            out_shape=shapes,
            in_specs=[smem if at < scalars else vmem for at in range(len(args))],
            out_specs=tuple(vmem for _ in shapes),
            scratch_shapes=scratch,
            compiler_params=pltpu.CompilerParams(vmem_limit_bytes=24 << 20),
        )(*args)

    return run


def trade(messages, count):
    whole = messages.reshape((count, -1) + messages.shape[1:])
    got = lax.all_to_all(whole, "chord", split_axis=0, concat_axis=0, tiled=True)
    return got.reshape(messages.shape)


def beside(up, down):
    size = lax.axis_size("span")
    low = lax.ppermute(up, "span", [(i, (i + 1) % size) for i in range(size)])
    high = lax.ppermute(down, "span", [(i, (i + size - 1) % size) for i in range(size)])
    return low, high


def local(
    velocity,
    pressure,
    viscosity,
    send_list,
    recv_slot,
    marker_block,
    marker_cells,
    marker_layer,
    marker_frac,
    marker_weights,
    marker_target,
    marker_count,
):
    count, strips = lax.axis_size("chord"), lax.axis_size("span")
    me = lax.axis_index("chord").astype(jnp.int32).reshape(1)
    at = lax.axis_index("span").astype(jnp.int32)
    send = send_list.T
    rim, spread, across = jnp.asarray(RIM), jnp.asarray(RIM.T), jnp.asarray(ACROSS)
    pack_flat, pack_rhs, pack_ext = jnp.asarray(PACK_FLAT), jnp.asarray(PACK_RHS), jnp.asarray(PACK_EXT)
    place, place_rhs, codes = jnp.asarray(PLACE), jnp.asarray(PLACE_RHS), jnp.asarray(CODES)
    mask, inside = jnp.asarray(MASK), jnp.asarray(INSIDE)

    plane, flat, rows = (SZ, 8, WIDTH), (SZ, 16, CELLS), (NB, SZ, CELLS)
    fans = (SZ, 8, LANES)
    vmem = lambda *shape: pltpu.VMEM(shape, F32)
    table, layers = vmem(16, SZ, LANES), vmem(SZ + 2 * DEPTH, 8, WIDTH)

    anywhere = pl.BlockSpec(memory_space=pl.ANY)
    messages = pl.pallas_call(
        first_pack,
        name="first_pack",
        out_shape=jax.ShapeDtypeStruct((2 * count, SZ, LANES), F32),
        in_specs=[anywhere] * 4,
        out_specs=pl.BlockSpec(memory_space=pltpu.VMEM),
        scratch_shapes=[
            pltpu.SMEM((2, count), jnp.int32),
            vmem(3 * NB, SZ, CELLS),
            vmem(NB, SZ, CELLS),
            pltpu.VMEM((CELLS, LANES), BF16),
            table,
            pltpu.SemaphoreType.DMA((4,)),
        ],
        compiler_params=pltpu.CompilerParams(vmem_limit_bytes=60 << 20),
    )(send, velocity.reshape(3 * NB, SZ, CELLS), pressure, rim)
    got = trade(messages, count)
    me, _ = lax.optimization_barrier((me, messages))
    route = pl.pallas_call(
        routes,
        name="routes",
        out_shape=jax.ShapeDtypeStruct((ROUTES,), jnp.int32),
        in_specs=[pl.BlockSpec(memory_space=pltpu.SMEM)] * 3,
        out_specs=pl.BlockSpec(memory_space=pltpu.SMEM),
        scratch_shapes=[pltpu.SMEM((32,), jnp.int32)],
    )(me, send, recv_slot)
    later, eddy, route = lax.optimization_barrier((velocity, viscosity, route))
    cells = jnp.concatenate([later, eddy[None]], axis=0)
    cells = jnp.transpose(cells, (2, 0, 1, 3)).reshape(SZ, 16, CELLS)
    cells_low, cells_high = beside(cells, cells)

    group = marker_block.shape[0] // strips
    groups = jnp.stack([at, (at + strips - 1) % strips])
    held = (CELLS, 2 * group)
    weights_high, weights_low, spans, aims = call(
        weigh, "weigh", [held, held, (16, 2 * group), (4, 2 * group)], [], 1, (BF16, BF16, F32, F32)
    )(
        groups, marker_block[None], marker_cells, marker_layer[None], marker_frac[None], marker_weights, marker_target
    )

    edge = (NB, RIMS + CELLS)
    rims, up, down = call(first_unpack, "first_unpack", [(SZ, 16, LANES), edge, edge], [], 1)(route, got, pressure)
    low, high = beside(up, down)
    tilde, total = call(own_layers, "own_layers", [flat, (16, 2 * group)], [], 0)(
        cells, cells_low, cells_high, rims, spread, weights_high, weights_low, spans
    )
    star, messages, up, down = call(
        forcing, "forcing", [flat, (count, 2, LANES), (NB, CELLS), (NB, CELLS)], [vmem(6, 16, CELLS), vmem(16, 1, LANES)], 2
    )(
        send, marker_count, cells, cells_low, cells_high, tilde, total, low, high, spread, rim, weights_high, weights_low, spans, aims
    )
    got = trade(messages, count)
    up, down, got = lax.optimization_barrier((up, down, got))
    star_low, star_high = beside(up, down)

    p, div, messages = call(
        first_step, "first_step", [rows, rows, (5 * count, SZ, LANES)],
        [vmem(SZ, 8, CELLS), vmem(4, NB, LANES), table, vmem(1, SZ, LANES), vmem(32, SZ, LANES)], 2,
    )(
        route, send, got, star, pressure, low, high, rims, spread, star_low, star_high, across, pack_flat, pack_rhs
    )
    got = trade(messages, count)
    edge = (SZ + REACH, NB, WIDTH + 2 * LANES)
    own, fan, div, up, down = call(
        middle_unpack, "middle_unpack", [plane, fans, plane, edge, edge],
        [vmem(SZ, 8, SEG + LANES), vmem(SZ, 8, SEG), vmem(2, SZ, 8, WIDTH)], 1,
    )(route, got, p, div, place, place_rhs)
    low, high = beside(up, down)
    p, rhs, messages = call(
        middle_sweeps, "middle_sweeps", [plane, (SZ + 2 * REACH, 8, WIDTH), (3 * count, SZ, LANES)],
        [layers, layers, vmem(NB, SZ, WIDTH), table, vmem(1, SZ, LANES)], 1,
    )(send, own, fan, low, high, div, mask, codes, pack_ext)
    got = trade(messages, count)
    edge = (SZ, NB, WIDTH + 2 * LANES)
    own, fan, up, down = call(
        last_unpack, "last_unpack", [plane, fans, edge, edge], [vmem(SZ, 8, SEG + LANES)], 1
    )(route, got, p, fan, place, inside)
    low, high = beside(up, down)
    velocity_next, pressure_next = call(
        last_sweeps, "last_sweeps", [(3 * NB, SZ, CELLS), rows], [layers, layers], 0
    )(own, fan, low, high, rhs, mask, codes, star)
    return velocity_next.reshape(velocity.shape), pressure_next


RIM = rim_matrix()
ACROSS = across_matrix()
PACK_FLAT = pack_matrix(CELLS, lambda i, k: EDGE * i + k)
PACK_RHS = pack_rhs_matrix()
PACK_EXT = pack_matrix(WIDTH, place_of)
PLACE = place_matrix()
PLACE_RHS = place_rhs_matrix()
CODES = fan_codes()
MASK = sheet_mask()
INSIDE = block_mask()


def solution(mesh):
    in_specs = (
        P(None, "chord", "span", None),
        P("chord", "span", None),
        P("chord", "span", None),
        P("chord", None),
        P("chord", None),
        P("chord"),
        P(None, "chord"),
        P("chord"),
        P("chord"),
        P(None, "chord"),
        P(None, "chord"),
        P("chord"),
    )
    out_specs = (P(None, "chord", "span", None), P("chord", "span", None))
    return jax.shard_map(local, mesh=mesh, in_specs=in_specs, out_specs=out_specs, check_vma=False)
```

```python
import math

import jax
import jax.numpy as jnp
import ml_dtypes
import numpy as np
from jax import lax
from jax.experimental import pallas as pl
from jax.experimental.pallas import tpu as pltpu
from jax.sharding import PartitionSpec as P

EDGE = 32
CELLS = EDGE * EDGE
NB = 4
SZ = 4
REACH = 3
DEPTH = 4
STRIDE = 40
WIDTH = 1664
LANES = 128
SEG = 4 * LANES
PATCH = ((0, 0), (0, 1), (1, 0), (0, 2), (1, 1), (2, 0))
F32 = jnp.float32
BF16 = jnp.bfloat16


def place_of(i, k):
    return STRIDE * (i + DEPTH) + k + 4


def edge_cell(side, depth, x):
    return [(depth, x), (EDGE - 1 - depth, x), (x, depth), (x, EDGE - 1 - depth)][side]


def ghost_cell(side, depth, x):
    return [(-1 - depth, x), (EDGE + depth, x), (x, -1 - depth), (x, EDGE + depth)][side]


def corner_cell(corner, i, k):
    return i if corner // 2 == 0 else EDGE - 1 - i, k if corner % 2 == 0 else EDGE - 1 - k


def vertex_cell(vertex, i=0, k=0):
    return -1 - i if vertex // 2 == 0 else EDGE + i, -1 - k if vertex % 2 == 0 else EDGE + k


def pack_matrix(rows, where):
    table = np.zeros((rows, SEG + LANES), np.float32)
    for side in range(4):
        for depth in range(DEPTH):
            for x in range(EDGE):
                table[where(*edge_cell(side, depth, x)), side * LANES + depth * EDGE + x] = 1
    for corner in range(4):
        for at, cell in enumerate(PATCH):
            table[where(*corner_cell(corner, *cell)), SEG + corner * 8 + at] = 1
    return table.astype(ml_dtypes.bfloat16)


def pack_rhs_matrix():
    table = np.zeros((CELLS, SEG), np.float32)
    for side in range(4):
        for depth in range(DEPTH - 1):
            for x in range(EDGE):
                i, k = edge_cell(side, depth, x)
                table[EDGE * i + k, side * LANES + depth * EDGE + x] = 1
        for corner in range(4):
            for at in range(4):
                i, k = corner_cell(corner, at // 2, at % 2)
                table[EDGE * i + k, side * LANES + 96 + corner * 4 + at] = 1
    return table.astype(ml_dtypes.bfloat16)


def place_matrix():
    table = np.zeros((SEG + LANES, WIDTH), np.float32)
    for side in range(4):
        for depth in range(DEPTH):
            for x in range(EDGE):
                table[side * LANES + depth * EDGE + x, place_of(*ghost_cell(side, depth, x))] = 1
    for vertex in range(4):
        for at, cell in enumerate(PATCH):
            table[SEG + vertex * 16 + at, place_of(*vertex_cell(vertex, *cell))] = 1
    return table.astype(ml_dtypes.bfloat16)


def place_rhs_matrix():
    table = np.zeros((SEG, WIDTH), np.float32)
    for side in range(4):
        for depth in range(DEPTH - 1):
            for x in range(EDGE):
                table[side * LANES + depth * EDGE + x, place_of(*ghost_cell(side, depth, x))] = 1
    for vertex in range(4):
        for at in range(3):
            table[vertex * LANES + 96 + at, place_of(*vertex_cell(vertex, at // 2, at % 2))] = 1
    return table.astype(ml_dtypes.bfloat16)


def across_matrix():
    table = np.zeros((LANES, CELLS), np.float32)
    for side in range(4):
        for x in range(EDGE):
            i, k = edge_cell(side, 0, x)
            table[side * EDGE + x, i * EDGE + k] = 0.5 if side % 2 else -0.5
    return table.astype(ml_dtypes.bfloat16)


def fan_codes():
    codes = np.zeros((8, WIDTH), np.float32)
    for vertex in range(4):
        to_i, to_k = 1 + (1 - vertex // 2), 3 + (1 - vertex % 2)
        codes[:NB, place_of(*vertex_cell(vertex))] = to_i
        codes[:NB, place_of(*vertex_cell(vertex, 0, 1))] = to_i + 4
        codes[NB:, place_of(*vertex_cell(vertex))] = to_k
        codes[NB:, place_of(*vertex_cell(vertex, 1, 0))] = to_k + 4
    return codes


def rim_matrix():
    table = np.zeros((CELLS, LANES), np.float32)
    for side in range(4):
        for x in range(EDGE):
            i, k = edge_cell(side, 0, x)
            table[i * EDGE + k, side * EDGE + x] = 1
    return table.astype(ml_dtypes.bfloat16)


def sheet_mask():
    mask = np.zeros((8, WIDTH), np.float32)
    for i in range(-DEPTH, EDGE + DEPTH):
        for k in range(-DEPTH, EDGE + DEPTH):
            inside_i, inside_k = 0 <= i < EDGE, 0 <= k < EDGE
            if inside_i and not inside_k:
                mask[:4, place_of(i, k)] = 1
            if inside_k and not inside_i:
                mask[4:, place_of(i, k)] = 1
    return mask


def block_mask():
    mask = np.zeros((8, WIDTH), np.float32)
    for i in range(EDGE):
        mask[:, place_of(i, 0) : place_of(i, 0) + EDGE] = 1
    return mask


def vertex_place(vertex):
    return place_of(*vertex_cell(vertex))


def pick(x, table):
    high = x.astype(BF16)
    rest = x - high.astype(F32)
    middle = rest.astype(BF16)
    low = (rest - middle.astype(F32)).astype(BF16)
    parts = jnp.dot(jnp.concatenate([high, middle, low], axis=0), table, preferred_element_type=F32)
    rows = x.shape[0]
    return (parts[:rows] + parts[rows : 2 * rows]) + parts[2 * rows :]


def shifted(x, lanes):
    return pltpu.roll(x, lanes % x.shape[1], axis=1)


def lane_ids(rows):
    return lax.broadcasted_iota(jnp.int32, (rows, LANES), 1)


def remap(x, width, pieces):
    rows = x.shape[0]
    lane = lane_ids(rows)
    out = []
    for tile in range(width // LANES):
        acc = jnp.zeros((rows, LANES), F32)
        base = tile * LANES
        for src, dst in pieces:
            first, last = max(dst, base), min(dst + EDGE, base + LANES)
            while first < last:
                at = src + first - dst
                column = at // LANES
                stop = min(last, first + (column + 1) * LANES - at)
                value = x[:, column * LANES : (column + 1) * LANES]
                turn = (first - base - at % LANES) % LANES
                if turn:
                    value = pltpu.roll(value, turn, axis=1)
                acc = jnp.where((lane >= first - base) & (lane < stop - base), value, acc)
                first = stop
        out.append(acc)
    return jnp.concatenate(out, axis=1)


def expand(x):
    return remap(x, WIDTH, [(EDGE * i, place_of(i, 0)) for i in range(EDGE)])


def compact(x):
    return remap(x, CELLS, [(place_of(i, 0), EDGE * i) for i in range(EDGE)])


def post(send_ref, out_ref, count, parts):
    units = len(parts)

    def one(target, carry):
        edges = [jnp.maximum(send_ref[slot, target], 0) for slot in range(2)]
        for unit, (table, slot, offset) in enumerate(parts):
            out_ref[target * units + unit] = table[offset if slot is None else offset + edges[slot]]
        return carry

    lax.fori_loop(0, count, one, 0, unroll=4)


def store_strips(strips, table_ref, corner_ref):
    lane = lane_ids(SZ)
    corners = jnp.zeros((SZ, LANES), F32)
    for block in range(NB):
        rows = strips[block * SZ : (block + 1) * SZ]
        for side in range(4):
            table_ref[block * 4 + side] = rows[:, side * LANES : (side + 1) * LANES]
        patch = rows[:, SEG:]
        patch = pltpu.roll(patch, EDGE * block, axis=1) if block else patch
        corners = jnp.where(lane // EDGE == block, patch, corners)
    corner_ref[0] = corners


def store_rhs_strips(strips, table_ref):
    lane = lane_ids(SZ)
    for side in range(4):
        parts = [strips[block * SZ : (block + 1) * SZ, side * LANES : (side + 1) * LANES] for block in range(NB)]
        for slot in range(2):
            patch = jnp.where(lane < 112, parts[2 * slot], pltpu.roll(parts[2 * slot + 1], 16, axis=1))
            for block in range(NB):
                table_ref[slot * 16 + block * 4 + side] = jnp.where(lane < 96, parts[block], patch)


def first_pack(
    send_any, velocity_any, p_any, rim_any, out_ref, send_ref, velocity_ref, p_ref, rim_ref, table_ref, done_ref
):
    pairs = ((velocity_any, velocity_ref), (rim_any, rim_ref), (p_any, p_ref), (send_any, send_ref))
    copies = [pltpu.make_async_copy(*pair, done_ref.at[at]) for at, pair in enumerate(pairs)]
    for copy in copies:
        copy.start()
    lane = lane_ids(SZ)
    for copy in copies:
        copy.wait()
    rows = [velocity_ref[...].reshape(3 * NB * SZ, CELLS), p_ref[...].reshape(NB * SZ, CELLS)]
    rims = pick(jnp.concatenate(rows, axis=0), rim_ref[...])
    for block in range(NB):
        for side in range(4):
            value = jnp.zeros((SZ, LANES), F32)
            for comp in range(4):
                first = (comp * NB + block) * SZ
                part = rims[first : first + SZ]
                turn = EDGE * (comp - side) % LANES
                if turn:
                    part = pltpu.roll(part, turn, axis=1)
                value = jnp.where(lane // EDGE == comp, part, value)
            table_ref[block * 4 + side] = value
    post(send_ref, out_ref, out_ref.shape[0] // 2, [(table_ref, 0, 0), (table_ref, 1, 0)])


def routes(me_ref, send_ref, recv_ref, out_ref, near_ref):
    me, count = me_ref[0], send_ref.shape[1]
    for edge in range(16):
        block, side = edge // 4, edge % 4
        entry = recv_ref[block, side]
        source, slot = entry // 2, entry % 2
        out_ref[2 * edge], out_ref[2 * edge + 1] = source, slot
        back = lax.rem(2 * me - source + count, count)
        near_ref[edge] = send_ref[slot, back] // 4
        near_ref[16 + edge] = lax.rem(source - me + count, count)
    for block in range(NB):
        for vertex in range(4):
            i_side, k_side = vertex // 2, 2 + vertex % 2
            for sheet, (side, then) in enumerate(((i_side, k_side), (k_side, i_side))):
                at, offset = block, 0
                for step, across in enumerate((side, then, side ^ 1, then ^ 1)):
                    edge = at * 4 + across
                    at, offset = near_ref[edge], offset + near_ref[16 + edge]
                    place = route_at(block, vertex, sheet, step)
                    out_ref[place] = lax.rem(me + offset, count)
                    out_ref[place + 1] = at


def route_at(block, vertex, sheet, step):
    return 32 + (((block * 4 + vertex) * 2 + sheet) * 4 + step) * 2


ROUTES = 32 + 32 * 8


def strip_of(got_ref, route_ref, block, side, unit, units):
    edge = block * 4 + side
    return got_ref[route_ref[2 * edge] * units + unit + route_ref[2 * edge + 1]]


def turned(rows, target, lane):
    return pltpu.roll(rows, lax.rem(target + LANES - lane, LANES), axis=1)


def gather_ghosts(got_ref, route_ref, ghost_ref, fan_ref, units, old_ref):
    lane = lane_ids(SZ)
    for block in range(NB):
        for side in range(4):
            strip = strip_of(got_ref, route_ref, block, side, 0, units)
            for sheet in range(2):
                ghost_ref[:, sheet * NB + block, side * LANES : (side + 1) * LANES] = strip
        for sheet in range(2):
            row = sheet * NB + block
            value = jnp.zeros((SZ, LANES), F32) if old_ref is None else old_ref[:, row, :]
            for vertex in range(4):
                far = (1 - vertex // 2) * 2 + 1 - vertex % 2
                beyond = far ^ 2 if sheet == 0 else far ^ 1
                first = vertex * 16

                def cells(step, corner, target, low, high, value):
                    place = route_at(block, vertex, sheet, step)
                    rows = got_ref[route_ref[place] * units + 2]
                    rows = turned(rows, target, route_ref[place + 1] * EDGE + corner * 8)
                    return jnp.where((lane >= low) & (lane < high), rows, value)

                value = cells(1, far, first, first, first + 6, value)
                value = cells(2, beyond, first + 6, first + 6, first + 9, value)
                value = cells(3, vertex, first + 9, first + 9, first + 10, value)
                if old_ref is None:
                    place = route_at(block, vertex, sheet, 2)
                    at = route_ref[place + 1]
                    rows = got_ref[route_ref[place] * units + 3 + at // 2]
                    rows = turned(rows, first + 10, 96 + (at % 2) * 16 + beyond * 4)
                    value = jnp.where(lane == first + 10, rows, value)
            ghost_ref[:, row, SEG:] = value
            fan_ref[:, row, :] = value


def gather_rhs(got_ref, route_ref, ghost_ref, units):
    lane = lane_ids(SZ)
    for block in range(NB):
        for vertex in range(4):
            strip = strip_of(got_ref, route_ref, block, vertex, 3, units)
            far = (1 - vertex // 2) * 2 + 1 - vertex % 2
            for sheet in range(2):
                place = route_at(block, vertex, sheet, 1)
                at = route_ref[place + 1]
                rows = got_ref[route_ref[place] * units + 3 + at // 2]
                rows = turned(rows, 96, (96 + (at % 2) * 16 + far * 4))
                value = jnp.where(lane < 96, strip, jnp.where(lane < 99, rows, 0.0))
                ghost_ref[:, sheet * NB + block, vertex * LANES : (vertex + 1) * LANES] = value


def moved(tiles, value, lane_from, place):
    tile, at = place // LANES, place % LANES
    turn = (at - lane_from) % LANES
    value = pltpu.roll(value, turn, axis=1) if turn else value
    tiles[tile] = jnp.where(lane_ids(value.shape[0]) == at, value, tiles[tile])


def tiles_of(x):
    return [x[:, at : at + LANES] for at in range(0, WIDTH, LANES)]


def fold(ext):
    last = [ext[:NB, WIDTH - LANES : WIDTH]]
    for vertex in range(4):
        place = vertex_place(vertex)
        tile = place // LANES * LANES
        moved(last, ext[NB:, tile : tile + LANES], place % LANES, 112 + vertex)
    return jnp.concatenate([ext[:NB, : WIDTH - LANES], last[0]], axis=1)


def unfold(rows):
    tiles = tiles_of(rows)
    last = tiles[-1]
    for vertex in range(4):
        moved(tiles, last, 112 + vertex, vertex_place(vertex))
    return jnp.concatenate([rows[:, :WIDTH], jnp.concatenate(tiles, axis=1)], axis=0)


def both_sheets(rows, corners):
    tiles = tiles_of(rows)
    if corners:
        segment = rows[:, WIDTH + LANES : WIDTH + 2 * LANES]
        for vertex in range(4):
            for at in range(3):
                moved(tiles, segment, vertex * 16 + at, place_of(*vertex_cell(vertex, *PATCH[at])))
    return jnp.concatenate([rows[:, :WIDTH], jnp.concatenate(tiles, axis=1)], axis=0)


def corner_tiles():
    cells = [vertex_cell(vertex, *cell) for vertex in range(4) for cell in PATCH[:3]]
    return sorted({place_of(*cell) // LANES for cell in cells})


def third_cells(fan):
    tiles = {tile: jnp.zeros((8, LANES), F32) for tile in corner_tiles()}
    for vertex in range(4):
        moved(tiles, fan, vertex * 16 + 6, vertex_place(vertex))
        moved(tiles, fan, vertex * 16 + 7, place_of(*vertex_cell(vertex, 0, 1)))
        moved(tiles, fan, vertex * 16 + 8, place_of(*vertex_cell(vertex, 1, 0)))
    return tiles


def third_sums(fan):
    total = (fan + shifted(fan, -1)) + (shifted(fan, -2) - shifted(fan, -3))
    tiles = {tile: jnp.zeros((8, LANES), F32) for tile in corner_tiles()}
    for vertex in range(4):
        moved(tiles, total, vertex * 16 + 7, vertex_place(vertex))
    return tiles


def merge(x, mask):
    return jnp.where(mask, pltpu.roll(x, NB, axis=0), x)


def second_halves(x):
    return jnp.concatenate([x, x], axis=0)


def first_unpack(recv_ref, got_ref, p_ref, rim_ref, up_ref, down_ref):
    lane = lane_ids(SZ)
    for block in range(NB):
        strips = [got_ref[recv_ref[block, side]] for side in range(4)]
        for comp in range(4):
            value = jnp.zeros((SZ, LANES), F32)
            for side in range(4):
                turn = EDGE * (side - comp) % LANES
                part = pltpu.roll(strips[side], turn, axis=1) if turn else strips[side]
                value = jnp.where(lane // EDGE == side, part, value)
            rim_ref[:, comp * NB + block, :] = value
    for layer in range(REACH):
        for comp in range(3):
            at = (layer * 3 + comp) * LANES
            up_ref[:, at : at + LANES] = rim_ref[layer + 1, comp * NB : (comp + 1) * NB, :]
            down_ref[:, at : at + LANES] = rim_ref[layer, comp * NB : (comp + 1) * NB, :]
    up_ref[:, RIMS:] = p_ref[:, SZ - 1, :]
    down_ref[:, RIMS:] = p_ref[:, 0, :]


RIMS = 3 * REACH * LANES


def send_planes(ext, fan, layer, up_ref, down_ref):
    for ref in (up_ref, down_ref):
        ref[layer, :, :WIDTH] = ext[:NB]
        ref[layer, :, WIDTH : WIDTH + LANES] = fan[:NB]
        ref[layer, :, WIDTH + LANES :] = fan[NB:]


def middle_unpack(
    route_ref, got_ref, p_ref, rhs_ref, place_ref, place_rhs_ref,
    own_ref, fan_ref, div_ref, up_ref, down_ref, ghost_ref, rhs_ghost_ref, block_ref,
):
    gather_ghosts(got_ref, route_ref, ghost_ref, fan_ref, 5, None)
    gather_rhs(got_ref, route_ref, rhs_ghost_ref, 5)
    placed = pick(ghost_ref[...].reshape(SZ * 8, SEG + LANES), place_ref[...])
    placed_rhs = pick(rhs_ghost_ref[...].reshape(SZ * 8, SEG), place_rhs_ref[...])
    for which, ref in enumerate((p_ref, rhs_ref)):
        whole = expand(ref[...].reshape(NB * SZ, CELLS))
        for block in range(NB):
            for sheet in range(2):
                block_ref[which, :, sheet * NB + block, :] = whole[block * SZ : (block + 1) * SZ]
    for layer in range(SZ):
        ext = block_ref[0, layer] + placed[layer * 8 : (layer + 1) * 8]
        own_ref[layer] = ext
        send_planes(ext, fan_ref[layer], layer, up_ref, down_ref)
        ext = block_ref[1, layer] + placed_rhs[layer * 8 : (layer + 1) * 8]
        div_ref[layer] = ext
        if layer >= 1:
            up_ref[SZ + layer - 1, :, :WIDTH] = fold(ext)
        if layer < SZ - 1:
            down_ref[SZ + layer, :, :WIDTH] = fold(ext)


def last_unpack(
    route_ref, got_ref, p_ref, old_ref, place_ref, block_ref, own_ref, fan_ref, up_ref, down_ref, ghost_ref
):
    gather_ghosts(got_ref, route_ref, ghost_ref, fan_ref, 3, old_ref)
    placed = pick(ghost_ref[...].reshape(SZ * 8, SEG + LANES), place_ref[...])
    for layer in range(SZ):
        ext = jnp.where(block_ref[...] > 0.0, p_ref[layer], 0.0) + placed[layer * 8 : (layer + 1) * 8]
        own_ref[layer] = ext
        send_planes(ext, fan_ref[layer], layer, up_ref, down_ref)


def rim_rows(ref, layer):
    rows = [ref[:, (3 * layer + comp) * LANES : (3 * layer + comp + 1) * LANES] for comp in range(3)]
    return jnp.concatenate(rows + [jnp.zeros((NB, LANES), F32)], axis=0)


def halves(x):
    high = x.astype(BF16)
    return high, (x - high.astype(F32)).astype(BF16)


def product(x, high, low, contract):
    rows = x.shape[0]
    dims = (((1,), (contract,)), ((), ()))
    parts = halves(x)
    both = lax.dot_general(jnp.concatenate(parts, axis=0), high, dims, preferred_element_type=F32)
    return (both[:rows] + both[rows:]) + lax.dot_general(parts[0], low, dims, preferred_element_type=F32)


def weigh(
    at_ref, block_ref, cells_ref, layer_ref, fraction_ref, weight_ref, target_ref, high_ref, low_ref, span_ref, aim_ref
):
    group = high_ref.shape[1] // 2
    along = lax.broadcasted_iota(jnp.int32, (EDGE, group), 0)
    for which in range(2):
        lanes = pl.ds(pl.multiple_of(at_ref[which] * group, group), group)
        here = slice(which * group, (which + 1) * group)
        corner = cells_ref[0:1, lanes]
        row_i, row_k = corner // EDGE, corner % EDGE
        weight = weight_ref[:, lanes]
        lines = []
        for a in range(4):
            line = jnp.zeros((EDGE, group), F32)
            for b in range(4):
                line = jnp.where(along == row_k + b, weight[4 * a + b : 4 * a + b + 1], line)
            lines.append(line)
        for i in range(EDGE):
            value = jnp.zeros((EDGE, group), F32)
            for a in range(4):
                value = jnp.where(row_i + a == i, lines[a], value)
            high, low = halves(value)
            high_ref[i * EDGE : (i + 1) * EDGE, here] = high
            low_ref[i * EDGE : (i + 1) * EDGE, here] = low
        start = layer_ref[:, lanes] - (at_ref[which] + which) * SZ
        fraction = fraction_ref[:, lanes]
        phi = [0.25 * (1.0 + jnp.cos(0.5 * math.pi * distance)) for distance in
               (1.0 + fraction, fraction, 1.0 - fraction, 2.0 - fraction)]
        for at in range(SZ + 2 * REACH):
            value = jnp.zeros((1, group), F32)
            for a in range(4):
                value = jnp.where(start + a == at - REACH, phi[a], value)
            span_ref[at : at + 1, here] = value
        aim_ref[0:3, here] = target_ref[:, lanes]
        aim_ref[3:4, here] = block_ref[:, lanes].astype(F32)


def diffused(cells_at, rims, spread, layer):
    cell = lax.broadcasted_iota(jnp.int32, (16, CELLS), 1)
    here = cells_at(layer)
    around = jnp.where(cell >= EDGE, shifted(here, EDGE), 0.0)
    around += jnp.where(cell < CELLS - EDGE, shifted(here, -EDGE), 0.0)
    around += jnp.where(cell % EDGE != 0, shifted(here, 1), 0.0)
    around += jnp.where(cell % EDGE != EDGE - 1, shifted(here, -1), 0.0)
    around += pick(rims, spread)
    around += cells_at(layer - 1) + cells_at(layer + 1)
    eddy = second_halves(second_halves(here[3 * NB :]))
    return here + eddy * (around - 6.0 * here)


def span_row(span_ref, layer):
    return span_ref[layer + REACH : layer + REACH + 1, :]


def layers_of(own_ref, low_ref, high_ref):
    def at(layer):
        if layer < 0:
            return low_ref[layer + SZ]
        return own_ref[layer] if layer < SZ else high_ref[layer - SZ]

    return at


def samples(tilde_ref, plane_high_ref, plane_low_ref, weights):
    dots = product(tilde_ref[...].reshape(len(weights) * 16, CELLS), plane_high_ref[...], plane_low_ref[...], 0)
    return sum(weight * dots[at * 16 : (at + 1) * 16] for at, weight in enumerate(weights))


def own_layers(
    own_ref, low_ref, high_ref, rim_ref, spread_ref, plane_high_ref, plane_low_ref, span_ref, tilde_ref, total_ref
):
    cells_at = layers_of(own_ref, low_ref, high_ref)
    for layer in range(SZ):
        tilde_ref[layer] = diffused(cells_at, rim_ref[layer], spread_ref[...], layer)
    total_ref[...] = samples(tilde_ref, plane_high_ref, plane_low_ref, [span_row(span_ref, layer) for layer in range(SZ)])


def forcing(
    send_ref, count_ref, own_ref, low_ref, high_ref, tilde_ref, total_ref, rim_low_ref, rim_high_ref, spread_ref,
    edge_ref, plane_high_ref, plane_low_ref, span_ref, aim_ref, star_ref, out_ref, up_ref, down_ref, beside_ref, table_ref,
):
    markers = plane_high_ref.shape[1]
    group = markers // 2
    cells_at = layers_of(own_ref, low_ref, high_ref)
    halo = [-3, -2, -1, SZ, SZ + 1, SZ + 2]
    for at, layer in enumerate(halo):
        rims = rim_rows(rim_low_ref, layer + SZ - 1) if layer < 0 else rim_rows(rim_high_ref, layer - SZ)
        beside_ref[at] = diffused(cells_at, rims, spread_ref[...], layer)
    total = total_ref[...] + samples(beside_ref, plane_high_ref, plane_low_ref, [span_row(span_ref, layer) for layer in halo])
    mine = (lax.broadcasted_iota(jnp.int32, (16, markers), 0) % NB).astype(F32) == aim_ref[3:4, :]
    total = jnp.where(mine, total, 0.0)
    place = lax.broadcasted_iota(jnp.int32, (1, markers), 1) % group
    live = place < count_ref[0]
    rows = []
    for comp in range(3):
        sampled = jnp.sum(total[comp * NB : (comp + 1) * NB], axis=0, keepdims=True)
        force = jnp.where(live, aim_ref[comp : comp + 1, :] - sampled, 0.0)
        rows.append(jnp.broadcast_to(force, (NB, markers)))
    rows.append(jnp.zeros((NB, markers), F32))
    force = jnp.where(mine, jnp.concatenate(rows, axis=0), 0.0)
    pushes = jnp.concatenate([span_row(span_ref, layer) * force for layer in range(SZ)], axis=0)
    spread = product(pushes, plane_high_ref[...], plane_low_ref[...], 1)
    star = tilde_ref[...].reshape(SZ * 16, CELLS) + spread
    star_ref[...] = star.reshape(SZ, 16, CELLS)
    up_ref[...] = star_ref[SZ - 1, 2 * NB : 3 * NB, :]
    down_ref[...] = star_ref[0, 2 * NB : 3 * NB, :]
    rims = pick(star, edge_ref[...])
    lane = lane_ids(NB)
    for side in range(4):
        value = jnp.zeros((NB, LANES), F32)
        for layer in range(SZ):
            row = layer * 16 + side // 2 * NB
            part = rims[row : row + NB]
            turn = EDGE * (layer - side) % LANES
            if turn:
                part = pltpu.roll(part, turn, axis=1)
            value = jnp.where(lane // EDGE == layer, part, value)
        for block in range(NB):
            table_ref[block * 4 + side] = value[block : block + 1]

    def one(target, carry):
        for slot in range(2):
            out_ref[target, slot : slot + 1, :] = table_ref[jnp.maximum(send_ref[slot, target], 0)]
        return carry

    lax.fori_loop(0, out_ref.shape[0], one, 0, unroll=4)


def half_step(star_ref, p_ref, low_ref, high_ref, rim_ref, spread_ref, out_ref):
    cell = lax.broadcasted_iota(jnp.int32, (NB, CELLS), 1)
    left, right = cell >= EDGE, cell < CELLS - EDGE
    front, back = cell % EDGE != 0, cell % EDGE != EDGE - 1
    rims = pick(jnp.concatenate([rim_ref[layer, 3 * NB :, :] for layer in range(SZ)], axis=0), spread_ref[...])

    def pressure_at(layer):
        if layer < 0:
            return low_ref[:, RIMS:]
        return p_ref[:, layer, :] if layer < SZ else high_ref[:, RIMS:]

    planes = [pressure_at(layer) for layer in range(-1, SZ + 1)]
    for layer in range(SZ):
        rows = star_ref[layer]
        first, second = rows[:NB], rows[NB : 2 * NB]
        flat = jnp.where(right, shifted(first, -EDGE), 0.0) - jnp.where(left, shifted(first, EDGE), 0.0)
        flat += jnp.where(back, shifted(second, -1), 0.0) - jnp.where(front, shifted(second, 1), 0.0)
        if layer < SZ - 1:
            flat += star_ref[layer + 1, 2 * NB : 3 * NB, :]
        if layer > 0:
            flat -= star_ref[layer - 1, 2 * NB : 3 * NB, :]
        out_ref[layer, :NB] = 0.5 * flat
        here = planes[layer + 1]
        around = jnp.where(left, shifted(here, EDGE), 0.0) + jnp.where(right, shifted(here, -EDGE), 0.0)
        around += jnp.where(front, shifted(here, 1), 0.0) + jnp.where(back, shifted(here, -1), 0.0)
        around += rims[layer * NB : (layer + 1) * NB] + (planes[layer] + planes[layer + 2])
        out_ref[layer, NB:] = around


def first_step(
    recv_ref, send_ref, got_ref, star_ref, pressure_ref, p_low_ref, p_high_ref, rim_ref, spread_ref,
    low_ref, high_ref, across_ref, pack_ref, pack_rhs_ref,
    p_ref, rhs_ref, out_ref, half_ref, near_ref, table_ref, corner_ref, rhs_table_ref,
):
    half_step(star_ref, pressure_ref, p_low_ref, p_high_ref, rim_ref, spread_ref, half_ref)
    lane = lane_ids(NB)
    for side in range(4):
        for block in range(NB):
            entry = recv_ref[block, side]
            rows = got_ref[entry // 2]
            near_ref[side, block : block + 1, :] = jnp.where(entry % 2 == 1, rows[1:2], rows[0:1])
    beyond = []
    for layer in range(SZ):
        value = jnp.zeros((NB, LANES), F32)
        for side in range(4):
            turn = EDGE * (side - layer) % LANES
            part = pltpu.roll(near_ref[side], turn, axis=1) if turn else near_ref[side]
            value = jnp.where(lane // EDGE == side, part, value)
        beyond.append(value)
    across = pick(jnp.concatenate(beyond, axis=0), across_ref[...])
    for layer in range(SZ):
        rhs = half_ref[layer, :NB, :] + across[layer * NB : (layer + 1) * NB]
        if layer == 0:
            rhs -= 0.5 * low_ref[...]
        if layer == SZ - 1:
            rhs += 0.5 * high_ref[...]
        rhs_ref[:, layer, :] = rhs
        p_ref[:, layer, :] = (half_ref[layer, NB:, :] - rhs) * (1.0 / 6.0)
    store_strips(pick(p_ref[...].reshape(NB * SZ, CELLS), pack_ref[...]), table_ref, corner_ref)
    store_rhs_strips(pick(rhs_ref[...].reshape(NB * SZ, CELLS), pack_rhs_ref[...]), rhs_table_ref)
    post(
        send_ref, out_ref, out_ref.shape[0] // 5,
        [(table_ref, 0, 0), (table_ref, 1, 0), (corner_ref, None, 0), (rhs_table_ref, 0, 0), (rhs_table_ref, 1, 16)],
    )


def sweep(source, target, step, rhs_ref, mask, codes, thirds):
    layers = SZ + 2 * DEPTH
    for at in range(step, layers - step):
        here = source[at]
        sides = [shifted(here, STRIDE), shifted(here, -STRIDE), shifted(here, 1), shifted(here, -1)]
        if at - DEPTH in thirds:
            for side in range(4):
                tiles = tiles_of(sides[side])
                for tile, cells in thirds[at - DEPTH].items():
                    code = codes[tile]
                    found = code == side + 1
                    if step == 1:
                        found = found | (code == side + 5)
                    tiles[tile] = jnp.where(found, cells, tiles[tile])
                sides[side] = jnp.concatenate(tiles, axis=1)
        around = (sides[0] + sides[1]) + (sides[2] + sides[3])
        around += source[at - 1] + source[at + 1]
        around -= rhs_ref[at - 1]
        target[at] = merge(around * (1.0 / 6.0), mask)


def load_layers(work_ref, own_ref, low_ref, high_ref):
    for layer in range(SZ):
        work_ref[layer] = both_sheets(low_ref[layer], layer >= 2)
        work_ref[DEPTH + layer] = own_ref[layer]
        work_ref[DEPTH + SZ + layer] = both_sheets(high_ref[layer], layer < 2)


def beside_segments(ref, layer):
    return jnp.concatenate([ref[layer, :, WIDTH : WIDTH + LANES], ref[layer, :, WIDTH + LANES :]], axis=0)


def sweeps(work_ref, other_ref, own_ref, fan_ref, low_ref, high_ref, rhs_ref, mask, codes, steps):
    load_layers(work_ref, own_ref, low_ref, high_ref)
    codes = tiles_of(codes)
    thirds = {layer: third_cells(fan_ref[layer]) for layer in range(SZ)}
    thirds[-1] = third_cells(beside_segments(low_ref, SZ - 1))
    thirds[SZ] = third_cells(beside_segments(high_ref, 0))
    later = {}
    for layer in range(SZ):
        later[layer] = {}
        for tile, total in third_sums(fan_ref[layer]).items():
            around = total + own_ref[layer, :, tile * LANES : (tile + 1) * LANES]
            later[layer][tile] = (around + (thirds[layer - 1][tile] + thirds[layer + 1][tile])) * (1.0 / 6.0)
    refs = (work_ref, other_ref)
    for step in range(1, steps + 1):
        given = thirds if step == 1 else later if step == 2 else {}
        sweep(refs[(step + 1) % 2], refs[step % 2], step, rhs_ref, mask, codes, given)
    return refs[steps % 2]


def middle_sweeps(
    send_ref, own_ref, fan_ref, low_ref, high_ref, div_ref, mask_ref, codes_ref, pack_ref,
    p_ref, rhs_ref, out_ref, work_ref, other_ref, rows_ref, table_ref, corner_ref,
):
    for layer in range(REACH):
        rhs_ref[layer] = unfold(low_ref[SZ + layer])
        rhs_ref[REACH + SZ + layer] = unfold(high_ref[SZ + layer])
    for layer in range(SZ):
        rhs_ref[REACH + layer] = div_ref[layer]
    done = sweeps(
        work_ref, other_ref, own_ref, fan_ref, low_ref, high_ref, rhs_ref, mask_ref[...] > 0.0, codes_ref[...], 4
    )
    for layer in range(SZ):
        here = done[DEPTH + layer]
        p_ref[layer] = here
        rows_ref[:, layer, :] = here[:NB]
    store_strips(pick(rows_ref[...].reshape(NB * SZ, WIDTH), pack_ref[...]), table_ref, corner_ref)
    post(
        send_ref, out_ref, out_ref.shape[0] // 3, [(table_ref, 0, 0), (table_ref, 1, 0), (corner_ref, None, 0)]
    )


def last_sweeps(
    own_ref, fan_ref, low_ref, high_ref, rhs_ref, mask_ref, codes_ref, star_ref, velocity_ref, p_ref, work_ref, other_ref
):
    done = sweeps(
        work_ref, other_ref, own_ref, fan_ref, low_ref, high_ref, rhs_ref, mask_ref[...] > 0.0, codes_ref[...], 3
    )
    for layer in range(SZ):
        here = done[DEPTH + layer]
        rows = [
            shifted(here, -STRIDE) - shifted(here, STRIDE),
            shifted(here, -1) - shifted(here, 1),
            done[DEPTH + layer + 1] - done[DEPTH + layer - 1],
            here,
        ]
        flat = compact(jnp.concatenate([row[:NB] for row in rows], axis=0))
        velocity_ref[:, layer, :] = (star_ref[layer] - 0.5 * flat)[: 3 * NB]
        p_ref[:, layer, :] = flat[3 * NB :]


def call(kernel, name, out_shapes, scratch, scalars, types=None):
    smem, vmem = pl.BlockSpec(memory_space=pltpu.SMEM), pl.BlockSpec(memory_space=pltpu.VMEM)
    types = types or (F32,) * len(out_shapes)
    shapes = tuple(jax.ShapeDtypeStruct(shape, held) for shape, held in zip(out_shapes, types))

    def run(*args):
        return pl.pallas_call(
            kernel,
            name=name,
            out_shape=shapes,
            in_specs=[smem if at < scalars else vmem for at in range(len(args))],
            out_specs=tuple(vmem for _ in shapes),
            scratch_shapes=scratch,
            compiler_params=pltpu.CompilerParams(vmem_limit_bytes=24 << 20),
        )(*args)

    return run


def trade(messages, count):
    whole = messages.reshape((count, -1) + messages.shape[1:])
    got = lax.all_to_all(whole, "chord", split_axis=0, concat_axis=0, tiled=True)
    return got.reshape(messages.shape)


def beside(up, down):
    size = lax.axis_size("span")
    low = lax.ppermute(up, "span", [(i, (i + 1) % size) for i in range(size)])
    high = lax.ppermute(down, "span", [(i, (i + size - 1) % size) for i in range(size)])
    return low, high


def local(
    velocity,
    pressure,
    viscosity,
    send_list,
    recv_slot,
    marker_block,
    marker_cells,
    marker_layer,
    marker_frac,
    marker_weights,
    marker_target,
    marker_count,
):
    count, strips = lax.axis_size("chord"), lax.axis_size("span")
    me = lax.axis_index("chord").astype(jnp.int32).reshape(1)
    at = lax.axis_index("span").astype(jnp.int32)
    send = send_list.T
    rim, spread, across = jnp.asarray(RIM), jnp.asarray(RIM.T), jnp.asarray(ACROSS)
    pack_flat, pack_rhs, pack_ext = jnp.asarray(PACK_FLAT), jnp.asarray(PACK_RHS), jnp.asarray(PACK_EXT)
    place, place_rhs, codes = jnp.asarray(PLACE), jnp.asarray(PLACE_RHS), jnp.asarray(CODES)
    mask, inside = jnp.asarray(MASK), jnp.asarray(INSIDE)

    plane, flat, rows = (SZ, 8, WIDTH), (SZ, 16, CELLS), (NB, SZ, CELLS)
    fans = (SZ, 8, LANES)
    vmem = lambda *shape: pltpu.VMEM(shape, F32)
    table, layers = vmem(16, SZ, LANES), vmem(SZ + 2 * DEPTH, 8, WIDTH)

    anywhere = pl.BlockSpec(memory_space=pl.ANY)
    messages = pl.pallas_call(
        first_pack,
        name="first_pack",
        out_shape=jax.ShapeDtypeStruct((2 * count, SZ, LANES), F32),
        in_specs=[anywhere] * 4,
        out_specs=pl.BlockSpec(memory_space=pltpu.VMEM),
        scratch_shapes=[
            pltpu.SMEM((2, count), jnp.int32),
            vmem(3 * NB, SZ, CELLS),
            vmem(NB, SZ, CELLS),
            pltpu.VMEM((CELLS, LANES), BF16),
            table,
            pltpu.SemaphoreType.DMA((4,)),
        ],
        compiler_params=pltpu.CompilerParams(vmem_limit_bytes=60 << 20),
    )(send, velocity.reshape(3 * NB, SZ, CELLS), pressure, rim)
    got = trade(messages, count)
    me, _ = lax.optimization_barrier((me, messages))
    route = pl.pallas_call(
        routes,
        name="routes",
        out_shape=jax.ShapeDtypeStruct((ROUTES,), jnp.int32),
        in_specs=[pl.BlockSpec(memory_space=pltpu.SMEM)] * 3,
        out_specs=pl.BlockSpec(memory_space=pltpu.SMEM),
        scratch_shapes=[pltpu.SMEM((32,), jnp.int32)],
    )(me, send, recv_slot)
    later, eddy, route = lax.optimization_barrier((velocity, viscosity, route))
    cells = jnp.concatenate([later, eddy[None]], axis=0)
    cells = jnp.transpose(cells, (2, 0, 1, 3)).reshape(SZ, 16, CELLS)
    cells_low, cells_high = beside(cells, cells)

    group = marker_block.shape[0] // strips
    groups = jnp.stack([at, (at + strips - 1) % strips])
    held = (CELLS, 2 * group)
    weights_high, weights_low, spans, aims = call(
        weigh, "weigh", [held, held, (16, 2 * group), (4, 2 * group)], [], 1, (BF16, BF16, F32, F32)
    )(
        groups, marker_block[None], marker_cells, marker_layer[None], marker_frac[None], marker_weights, marker_target
    )

    edge = (NB, RIMS + CELLS)
    rims, up, down = call(first_unpack, "first_unpack", [(SZ, 16, LANES), edge, edge], [], 1)(recv_slot, got, pressure)
    low, high = beside(up, down)
    tilde, total = call(own_layers, "own_layers", [flat, (16, 2 * group)], [], 0)(
        cells, cells_low, cells_high, rims, spread, weights_high, weights_low, spans
    )
    star, messages, up, down = call(
        forcing, "forcing", [flat, (count, 2, LANES), (NB, CELLS), (NB, CELLS)], [vmem(6, 16, CELLS), vmem(16, 1, LANES)], 2
    )(
        send, marker_count, cells, cells_low, cells_high, tilde, total, low, high, spread, rim, weights_high, weights_low, spans, aims
    )
    got = trade(messages, count)
    up, down, got = lax.optimization_barrier((up, down, got))
    star_low, star_high = beside(up, down)

    p, div, messages = call(
        first_step, "first_step", [rows, rows, (5 * count, SZ, LANES)],
        [vmem(SZ, 8, CELLS), vmem(4, NB, LANES), table, vmem(1, SZ, LANES), vmem(32, SZ, LANES)], 2,
    )(
        recv_slot, send, got, star, pressure, low, high, rims, spread, star_low, star_high, across, pack_flat, pack_rhs
    )
    got = trade(messages, count)
    edge = (SZ + REACH, NB, WIDTH + 2 * LANES)
    own, fan, div, up, down = call(
        middle_unpack, "middle_unpack", [plane, fans, plane, edge, edge],
        [vmem(SZ, 8, SEG + LANES), vmem(SZ, 8, SEG), vmem(2, SZ, 8, WIDTH)], 1,
    )(route, got, p, div, place, place_rhs)
    low, high = beside(up, down)
    p, rhs, messages = call(
        middle_sweeps, "middle_sweeps", [plane, (SZ + 2 * REACH, 8, WIDTH), (3 * count, SZ, LANES)],
        [layers, layers, vmem(NB, SZ, WIDTH), table, vmem(1, SZ, LANES)], 1,
    )(send, own, fan, low, high, div, mask, codes, pack_ext)
    got = trade(messages, count)
    edge = (SZ, NB, WIDTH + 2 * LANES)
    own, fan, up, down = call(
        last_unpack, "last_unpack", [plane, fans, edge, edge], [vmem(SZ, 8, SEG + LANES)], 1
    )(route, got, p, fan, place, inside)
    low, high = beside(up, down)
    velocity_next, pressure_next = call(
        last_sweeps, "last_sweeps", [(3 * NB, SZ, CELLS), rows], [layers, layers], 0
    )(own, fan, low, high, rhs, mask, codes, star)
    return velocity_next.reshape(velocity.shape), pressure_next


RIM = rim_matrix()
ACROSS = across_matrix()
PACK_FLAT = pack_matrix(CELLS, lambda i, k: EDGE * i + k)
PACK_RHS = pack_rhs_matrix()
PACK_EXT = pack_matrix(WIDTH, place_of)
PLACE = place_matrix()
PLACE_RHS = place_rhs_matrix()
CODES = fan_codes()
MASK = sheet_mask()
INSIDE = block_mask()


def solution(mesh):
    in_specs = (
        P(None, "chord", "span", None),
        P("chord", "span", None),
        P("chord", "span", None),
        P("chord", None),
        P("chord", None),
        P("chord"),
        P(None, "chord"),
        P("chord"),
        P("chord"),
        P(None, "chord"),
        P(None, "chord"),
        P("chord"),
    )
    out_specs = (P(None, "chord", "span", None), P("chord", "span", None))
    return jax.shard_map(local, mesh=mesh, in_specs=in_specs, out_specs=out_specs, check_vma=False)
```
